128 devices in a mesh: face: 8 (over y, core), elem: 16 (over z, x).
Axes of the slice: x: 4, y: 4, z: 4, core: 2. Of those that a mesh axis runs over, the one named last changes fastest.
Arguments:
- amount: float32 [24, 32768], P(None, ('face', 'elem')), may hold values from 0.05 to 1
- scatter: float32 [24, 32768], P(None, ('face', 'elem')), may hold values from 0.02 to 0.6
- cloud_path: float32 [24, 32768], P(None, ('face', 'elem')), may hold values from 0.01 to 1
- planck: float32 [24, 32768], P(None, ('face', 'elem')), may hold values from 0.4 to 1.6
- thickness: float32 [24, 32768], P(None, ('face', 'elem')), may hold values from 0.5 to 2
- corner_weights: float32 [8, 24, 32768], P(None, None, ('face', 'elem')), may hold values from 0 to 1, as said below
- table_index: int32 [24, 32768], P(None, ('face', 'elem')), may hold values from 0 to 6658, as said below
- cosine: float32 [32768], P(('face', 'elem')), may hold values from 0.1 to 1
- albedo: float32 [32768], P(('face', 'elem')), may hold values from 0.05 to 0.6
- surface_source: float32 [32768], P(('face', 'elem')), may hold values from 0.8 to 1.6
- stretch_map: int32 [32768], replicated, may hold values from 0 to 32767, as said below
- sunlit: int32 [256], P(('face', 'elem')), may hold values from 0 to 1, as said below
- table_longwave: bfloat16 [7560, 256], replicated, may hold values from 0.0099487305 to 2
- table_shortwave: bfloat16 [7560, 224], replicated, may hold values from 0.0049743652 to 1
- cloud_longwave: float32 [256], replicated, may hold values from 0.05 to 2
- cloud_shortwave: float32 [224], replicated, may hold values from 0.05 to 2
- planck_fraction: float32 [256], replicated, may hold values from 0.3 to 3
- rayleigh: float32 [224], replicated, may hold values from 0.05 to 1
- solar_flux: float32 [224], replicated, may hold values from 0.3 to 3
Outputs:
- heating_longwave: float32 [24, 32768], P(None, ('face', 'elem'))
- heating_shortwave: float32 [24, 32768], P(None, ('face', 'elem'))
The draws below stay inside these ranges and needn't reach their ends.
Inputs may be any that keep to these rules, and one draw needn't show every extreme that they name: `stretch_map`: A permutation: each device's 256 dynamics columns hold exactly 2 positions in each device's range of 256 physics positions. Exactly 128 blocks are sunlit; in every draw some device has all its 2 blocks sunlit. table_index = e * 14 * 60 + t * 60 + p with e < 8, t < 13, p < 59. `corner_weights`: trilinear weights: corner 4 e + 2 t + p is the product of the three fractions or their complements; the eight of a level sum to one.
All inputs are finite; a program needn't handle non-finite values.
Results may differ from the reference program's by a relative error of at most 0.0011.
Values sent between devices are 32-bit elements; how exact they have to be, the bound alone decides.
A program may use at most 64 MiB of HBM per device.

```python
import math
import jax
import jax.numpy as jnp
from jax import lax

L = 24
G_LW = 256
G_SW = 224
NT_ETA = 9
NT_TEMP = 14
NT_PRES = 60
BLOCK = 128
COL_DEV = 256
COLUMNS = 32768
BLK_DEV = 2
NBLK = 256
NTAB = 7560


def draw_stretch_map(key, part):
    key = jax.random.fold_in(key, 3)
    devices = COLUMNS // COL_DEV
    per_peer = COL_DEV // devices
    keys_all = jax.random.split(key, 2 * devices)
    source_perm = jax.vmap(lambda subkey: jax.random.permutation(subkey, COL_DEV))(keys_all[:devices]).astype(jnp.int32)
    target_perm = jax.vmap(lambda subkey: jax.random.permutation(subkey, COL_DEV))(keys_all[devices:]).astype(jnp.int32)
    target = source_perm // per_peer
    within = source_perm % per_peer
    sender = jnp.arange(devices, dtype=jnp.int32)[:, None]
    slot_index = target_perm[target, sender * per_peer + within]
    return (target * COL_DEV + slot_index).reshape(COLUMNS).astype(jnp.int32)


def draw_table_index(key, part):
    key = jax.random.fold_in(key, 5)
    key_eta, key_temp, key_pres = jax.random.split(key, 3)
    eta_row = jax.random.randint(key_eta, (L, COLUMNS), 0, NT_ETA - 1)
    temp_row = jax.random.randint(key_temp, (L, COLUMNS), 0, NT_TEMP - 1)
    pres_row = jax.random.randint(key_pres, (L, COLUMNS), 0, NT_PRES - 1)
    return (eta_row * NT_TEMP * NT_PRES + temp_row * NT_PRES + pres_row).astype(jnp.int32)


def draw_corner_weights(key, part):
    key = jax.random.fold_in(key, 7)
    fractions = jax.random.uniform(key, (3, L, COLUMNS), jnp.float32)
    corners = []
    for corner in range(8):
        eta_part = fractions[0] if corner // 4 else 1.0 - fractions[0]
        temp_part = fractions[1] if corner // 2 % 2 else 1.0 - fractions[1]
        pres_part = fractions[2] if corner % 2 else 1.0 - fractions[2]
        corners.append(eta_part * temp_part * pres_part)
    return jnp.stack(corners).astype(jnp.float32)


def draw_sunlit(key, part):
    key = jax.random.fold_in(key, 11)
    devices = NBLK // BLK_DEV
    key_device, key_rank = jax.random.split(key)
    chosen = jax.random.randint(key_device, (), 0, devices)
    priority = jax.random.permutation(key_rank, NBLK).astype(jnp.int32)
    owner = jnp.arange(NBLK, dtype=jnp.int32) // BLK_DEV
    priority = jnp.where(owner == chosen, -1, priority)
    ranking = jnp.argsort(jnp.argsort(priority, stable=True), stable=True)
    return (ranking < NBLK // 2).astype(jnp.int32)


def shard_levels(key, dims, shards, low, largest):
    def one(axis_at, parts):
        draws = jax.random.uniform(jax.random.fold_in(jax.random.fold_in(key, 6), axis_at), (parts,), jnp.float32, low / len(shards), largest / len(shards))
        return jnp.repeat(jnp.exp(draws), dims[axis_at] // parts).reshape((-1,) + (1,) * (len(dims) - axis_at - 1))

    gain = one(*shards[0])
    for cut in shards[1:]:
        gain = gain * one(*cut)
    return gain


def setup_inputs(seed: int = 0) -> dict:
    key_list = jax.random.split(jax.random.key(seed), 20)
    amount = jnp.clip(jnp.exp(math.log(1.0) - 2.9957323 * jax.random.uniform(key_list[0], (L, COLUMNS), jnp.float32) ** shard_levels(key_list[0], (L, COLUMNS), ((1, 128),), -0.2, 0.2)), 0.05, 1.0)
    scatter = jnp.clip(jnp.exp(math.log(0.6) - 3.4011974 * jax.random.uniform(key_list[1], (L, COLUMNS), jnp.float32) ** shard_levels(key_list[1], (L, COLUMNS), ((1, 128),), -0.2, 0.2)), 0.02, 0.6)
    cloud_path = jnp.clip(jnp.exp(math.log(1.0) - 4.6051702 * jax.random.uniform(key_list[2], (L, COLUMNS), jnp.float32) ** shard_levels(key_list[2], (L, COLUMNS), ((1, 128),), -0.2, 0.2)), 0.01, 1.0)
    planck = jnp.clip(0.4 + 1.2 * jax.random.uniform(key_list[3], (L, COLUMNS), jnp.float32) ** shard_levels(key_list[3], (L, COLUMNS), ((1, 128),), -0.2, 0.2), 0.4, 1.6)
    thickness = jnp.clip(jnp.exp(math.log(2.0) - 1.3862944 * jax.random.uniform(key_list[4], (L, COLUMNS), jnp.float32) ** shard_levels(key_list[4], (L, COLUMNS), ((1, 128),), -0.2, 0.2)), 0.5, 2.0)
    corner_weights = draw_corner_weights(jax.random.fold_in(key_list[19], 71), 0)
    table_index = draw_table_index(jax.random.fold_in(key_list[19], 71), 0)
    cosine = jnp.clip(0.1 + 0.9 * jax.random.uniform(key_list[7], (COLUMNS,), jnp.float32) ** shard_levels(key_list[7], (COLUMNS,), ((0, 128),), -0.2, 0.2), 0.1, 1.0)
    albedo = jnp.clip(0.05 + 0.55 * jax.random.uniform(key_list[8], (COLUMNS,), jnp.float32) ** shard_levels(key_list[8], (COLUMNS,), ((0, 128),), -0.2, 0.2), 0.05, 0.6)
    surface_source = jnp.clip(0.8 + 0.8 * jax.random.uniform(key_list[9], (COLUMNS,), jnp.float32) ** shard_levels(key_list[9], (COLUMNS,), ((0, 128),), -0.2, 0.2), 0.8, 1.6)
    stretch_map = draw_stretch_map(jax.random.fold_in(key_list[19], 71), 0)
    sunlit = draw_sunlit(jax.random.fold_in(key_list[19], 71), 0)
    table_longwave = jnp.clip(jnp.exp(jax.random.uniform(key_list[12], (NTAB, G_LW), jnp.float32, math.log(0.0099487305), math.log(2.0))), 0.0099487305, 2.0).astype(jnp.bfloat16)
    table_shortwave = jnp.clip(jnp.exp(jax.random.uniform(key_list[13], (NTAB, G_SW), jnp.float32, math.log(0.0049743652), math.log(1.0))), 0.0049743652, 1.0).astype(jnp.bfloat16)
    cloud_longwave = jnp.clip(jnp.exp(jax.random.uniform(key_list[14], (G_LW,), jnp.float32, math.log(0.05), math.log(2.0))), 0.05, 2.0)
    cloud_shortwave = jnp.clip(jnp.exp(jax.random.uniform(key_list[15], (G_SW,), jnp.float32, math.log(0.05), math.log(2.0))), 0.05, 2.0)
    planck_fraction = jnp.clip(jnp.exp(jax.random.uniform(key_list[16], (G_LW,), jnp.float32, math.log(0.3), math.log(3.0))), 0.3, 3.0)
    rayleigh = jnp.clip(jnp.exp(jax.random.uniform(key_list[17], (G_SW,), jnp.float32, math.log(0.05), math.log(1.0))), 0.05, 1.0)
    solar_flux = jnp.clip(jnp.exp(jax.random.uniform(key_list[18], (G_SW,), jnp.float32, math.log(0.3), math.log(3.0))), 0.3, 3.0)
    return {"amount": amount, "scatter": scatter, "cloud_path": cloud_path, "planck": planck, "thickness": thickness, "corner_weights": corner_weights, "table_index": table_index, "cosine": cosine, "albedo": albedo, "surface_source": surface_source, "stretch_map": stretch_map, "sunlit": sunlit, "table_longwave": table_longwave, "table_shortwave": table_shortwave, "cloud_longwave": cloud_longwave, "cloud_shortwave": cloud_shortwave, "planck_fraction": planck_fraction, "rayleigh": rayleigh, "solar_flux": solar_flux}


diffusivity = 1.66


def chain(factor, offset, start, backward):
    def stepper(carry, pair):
        following = pair[0] * carry + pair[1]
        return following, following

    _, result = lax.scan(stepper, start, (factor, offset), reverse=backward)
    return result


def lookup(weights, index, gas_table):
    plane_size = NT_TEMP * NT_PRES
    rounded = lax.optimization_barrier(weights.astype(jnp.bfloat16)).astype(jnp.float32)
    table_full = gas_table.astype(jnp.float32)
    total = jnp.zeros(index.shape + (gas_table.shape[1],), jnp.float32)
    for corner in range(8):
        offset = (corner // 4) * plane_size + ((corner // 2) % 2) * NT_PRES + corner % 2
        picked = jnp.take(table_full, (index + offset).astype(jnp.int32), axis=0)
        total = total + rounded[corner][:, :, None] * picked
    return total


def longwave(kappa, amount, cloud_path, planck, thickness, surface_source, cloud_longwave, planck_fraction):
    depth = amount[:, :, None] * kappa + cloud_path[:, :, None] * cloud_longwave
    transmit = jnp.exp(-diffusivity * depth)
    emitted = (1.0 - transmit) * (planck[:, :, None] * planck_fraction)
    bottom = surface_source[:, None] * planck_fraction
    zeros_top = jnp.zeros_like(bottom)
    downward = chain(transmit, emitted, zeros_top, False)
    upward = chain(transmit, emitted, bottom, True)
    net_upper = upward - jnp.concatenate([zeros_top[None], downward[:-1]], axis=0)
    net_lower = jnp.concatenate([upward[1:], bottom[None]], axis=0) - downward
    return jnp.sum(net_lower - net_upper, axis=2) / (planck_fraction.shape[0] * thickness)


def shortwave(kappa, amount, scatter, cloud_path, thickness, cosine, albedo, rayleigh, cloud_shortwave, solar_flux):
    absorbed = amount[:, :, None] * kappa
    scattered = scatter[:, :, None] * rayleigh + cloud_path[:, :, None] * cloud_shortwave
    extinct = absorbed + scattered
    beam = jnp.exp(-extinct / cosine[None, :, None])
    spread = jnp.exp(-diffusivity * (absorbed + 0.5 * scattered))
    top_flux = cosine[:, None] * solar_flux
    zeros_top = jnp.zeros_like(top_flux)
    below = chain(beam, jnp.zeros_like(beam), top_flux, False)
    direct = jnp.concatenate([top_flux[None], below[:-1]], axis=0)
    source = 0.5 * direct * (1.0 - beam) * scattered / extinct
    downward = chain(spread, source, zeros_top, False)
    bottom = albedo[:, None] * (below[-1] + downward[-1])
    upward = chain(spread, source, bottom, True)
    net_upper = upward - jnp.concatenate([zeros_top[None], downward[:-1]], axis=0) - direct
    net_lower = jnp.concatenate([upward[1:], bottom[None]], axis=0) - downward - below
    return jnp.sum(net_lower - net_upper, axis=2) / (solar_flux.shape[0] * thickness)


def reference(amount, scatter, cloud_path, planck, thickness, corner_weights, table_index, cosine, albedo, surface_source, stretch_map, sunlit, table_longwave, table_shortwave, cloud_longwave, cloud_shortwave, planck_fraction, rayleigh, solar_flux):
    positions = jnp.arange(COLUMNS, dtype=jnp.int32)
    inverse = jnp.zeros((COLUMNS,), jnp.int32).at[stretch_map.astype(jnp.int32)].set(positions)
    fields = [jnp.take(field, inverse, axis=-1) for field in (amount, scatter, cloud_path, planck, thickness, cosine, albedo, surface_source)]

    def per_block(block):
        start = (block * BLOCK).astype(jnp.int32)

        def cut_out(array):
            return lax.dynamic_slice_in_dim(array, start, BLOCK, array.ndim - 1)

        p_amount, p_scatter, p_cloud, p_planck, p_thickness, p_cosine, p_albedo, p_surface = [cut_out(field) for field in fields]
        weights_cut = cut_out(corner_weights)
        index_cut = cut_out(table_index)
        heat_long = longwave(lookup(weights_cut, index_cut, table_longwave), p_amount, p_cloud, p_planck, p_thickness, p_surface, cloud_longwave, planck_fraction)
        flag = lax.dynamic_index_in_dim(sunlit, block, keepdims=False).astype(jnp.float32)
        heat_short = shortwave(lookup(weights_cut, index_cut, table_shortwave), p_amount, p_scatter, p_cloud, p_thickness, p_cosine, p_albedo, rayleigh, cloud_shortwave, solar_flux) * flag
        return heat_long, heat_short

    long_blocks, short_blocks = lax.map(per_block, jnp.arange(NBLK, dtype=jnp.int32))
    long_phys = jnp.moveaxis(long_blocks, 0, 1).reshape(L, COLUMNS)
    short_phys = jnp.moveaxis(short_blocks, 0, 1).reshape(L, COLUMNS)
    return jnp.take(long_phys, stretch_map, axis=1), jnp.take(short_phys, stretch_map, axis=1)
```

```python
import functools
import math
import jax
import jax.numpy as jnp
from jax import lax
from jax.experimental import pallas as pl
from jax.experimental.pallas import tpu as pltpu
from jax.sharding import PartitionSpec as P

LEVELS = 24
NT_TEMP = 14
NT_PRES = 60
NTAB = 7560
COLS = 256
PEERS = 128
FULL = NTAB // 16 * 16
SCALE = -0.83 / math.log(2.0)
CORNERS = tuple(4 * (e * NT_TEMP * NT_PRES + t * NT_PRES) for e in range(2) for t in range(2))
GROUP = 32
WIDE = 16


def iota(shape, axis):
    return lax.broadcasted_iota(jnp.int32, shape, axis)


def parts(x):
    high = x.astype(jnp.bfloat16)
    rest = x - high.astype(jnp.float32)
    middle = rest.astype(jnp.bfloat16)
    low = (rest - middle.astype(jnp.float32)).astype(jnp.bfloat16)
    return (low, middle, high)


def pick(chooser, x, contract=0):
    total = None
    for part in parts(x):
        term = lax.dot_general(
            chooser, part, (((1,), (contract,)), ((), ())), preferred_element_type=jnp.float32
        )
        total = term if total is None else total + term
    return total


def as_row(pair):
    return jnp.concatenate([pair[0:1], pair[1:2]], axis=1)


def eye():
    return iota((COLS, COLS), 0) == iota((COLS, COLS), 1)


def to_column(row):
    return jnp.sum(jnp.where(eye(), row, 0.0), axis=1, keepdims=True)


def to_row(column):
    return jnp.sum(jnp.where(eye(), column, 0.0), axis=0, keepdims=True)


def onehot(mask):
    return jnp.where(mask, 1.0, 0.0).astype(jnp.bfloat16)


def slots_of(targets):
    target_row = as_row(targets)
    owner = (target_row >> 8).astype(jnp.float32)
    position = (target_row & 255).astype(jnp.float32)
    earlier = (to_column(owner) == owner) & (iota((COLS, COLS), 0) < iota((COLS, COLS), 1))
    rank = jnp.sum(jnp.where(earlier, 1.0, 0.0), axis=0, keepdims=True)
    return 2.0 * owner + rank, position


def fill_table(long_in, short_in, table):
    def long_rows(base, count):
        rows = long_in[pl.ds(base, count), :].astype(jnp.float32) * 2.0
        table[pl.ds(base * 4, count, 4), :] = rows[:, :128]
        table[pl.ds(base * 4 + 1, count, 4), :] = rows[:, 128:]

    def long_body(step, carry):
        for inner in range(8):
            long_rows(pl.multiple_of(step * 128, 128) + inner * 16, 16)
        return carry

    lax.fori_loop(0, FULL // 128, long_body, 0)
    long_rows(FULL, NTAB - FULL)

    def short_rows(block, base, count):
        unit = onehot(iota((count, count), 0) == iota((count, count), 1))
        rows = lax.dot_general(
            unit, block, (((1,), (1,)), ((), ())), preferred_element_type=jnp.float32
        )
        table[pl.ds(base * 4 + 2, count, 4), :] = rows[:, :128]
        table[pl.ds(base * 4 + 3, count, 4), :] = rows[:, 128:]

    def short_body(step, carry):
        base = pl.multiple_of(step * 256, 256)
        short_rows(short_in[:, pl.ds(base, 256)], base, 256)
        return carry

    short_in[224:256, :] = jnp.zeros((32, NTAB), jnp.bfloat16)
    lax.fori_loop(0, NTAB // 256, short_body, 0)
    short_rows(short_in[:, FULL - 128:FULL], FULL - 128, 128)
    short_rows(short_in[:, FULL:NTAB], FULL, NTAB - FULL)


def spread_weights(weights, lanes):
    source, lane = iota((64, 256), 0), iota((64, 256), 1)
    expand = onehot((source // 8 == (lane // 4) % 8) & (source % 8 == lane // 32))
    for third in range(3):
        low = weights[:, third * 8:third * 8 + 8, :].reshape(64, COLS).astype(jnp.bfloat16)
        lanes[third * COLS:(third + 1) * COLS, :] = lax.dot_general(
            low, expand, (((0,), (0,)), ((), ())), preferred_element_type=jnp.float32
        )


def gather(rows, table, lanes, kappa):
    out_row, lane = iota((32, 256), 0), iota((32, 256), 1)
    mask = (out_row // 4 == lane // 32) & (out_row % 4 == lane % 4)

    def body(step, carry):
        third = step // (COLS // GROUP)
        first = step % (COLS // GROUP) * GROUP
        for member in range(GROUP):
            place = step * GROUP + member
            picked = []
            for level in range(8):
                base = rows[third * 8 + level, first + member]
                for corner in CORNERS:
                    picked.append(table[pl.ds(base + corner, 8), :])
            right = jnp.concatenate(picked, axis=0).astype(jnp.bfloat16)
            weight = jnp.broadcast_to(lanes[pl.ds(place, 1), :], (32, 256))
            left = jnp.where(mask, weight, 0.0).astype(jnp.bfloat16)
            kappa[pl.ds(pl.multiple_of(place * 32, 32), 32), :] = jnp.dot(
                left, right, preferred_element_type=jnp.float32
            )
        return carry

    lax.fori_loop(0, 3 * COLS // GROUP, body, 0)


def radiate(state, kappa, heat, lit, params, held):
    cloud_long, planck_part, cloud_short, ray, flux = params
    lane = iota((WIDE, 128), 1)

    def body(step, carry):
        start = pl.multiple_of(step * WIDE, WIDE)
        fields = state[pl.ds(start, WIDE), :]
        scaled = fields * SCALE

        def wide(x, at):
            return jnp.broadcast_to(x[:, at:at + 1], (WIDE, 128))

        cosine = wide(fields, 120)
        albedo = wide(fields, 121)
        surface = wide(fields, 122)
        path = (1.0 / 0.83) / cosine
        down = [jnp.zeros((WIDE, 128), jnp.float32) for _ in range(2)]
        sdown = [jnp.zeros((WIDE, 128), jnp.float32) for _ in range(2)]
        direct = [jnp.ones((WIDE, 128), jnp.float32) for _ in range(2)]
        for level in range(LEVELS):
            amount = wide(scaled, 24 + level)
            scatter = wide(scaled, 48 + level)
            cloud = wide(scaled, 72 + level)
            planck = wide(fields, 96 + level)
            origin = (level // 8 * COLS + start) * 32 + level % 8 * 4
            for half in range(2):
                value = kappa[pl.ds(origin + half, WIDE, 32), :]
                absorb = 1.0 - jnp.exp2(amount * value + cloud * cloud_long[half])
                gain = absorb * (planck - down[half])
                down[half] = down[half] + gain
                held[level, half] = absorb
                held[level, 2 + half] = gain
            for half in range(2):
                value = kappa[pl.ds(origin + 2 + half, WIDE, 32), :]
                absorbed = amount * value
                scattered = scatter * ray[half] + cloud * cloud_short[half]
                extinct = absorbed + scattered
                lost = direct[half] * (1.0 - jnp.exp2(extinct * path))
                direct[half] = direct[half] - lost
                kept = lost * (absorbed / extinct)
                source = 0.5 * (lost - kept)
                close = 1.0 - jnp.exp2(extinct + absorbed)
                taken = close * sdown[half]
                sdown[half] = sdown[half] - taken + source
                held[level, 4 + half] = close
                held[level, 6 + half] = source
                held[level, 8 + half] = taken + kept
        up = [surface, surface]
        sup = [albedo * (direct[half] + sdown[half]) for half in range(2)]
        result = jnp.zeros((WIDE, 128), jnp.float32)
        for level in reversed(range(LEVELS)):
            planck = wide(fields, 96 + level)
            long_sum, short_sum = None, None
            for half in range(2):
                gain = held[level, half] * (planck - up[half])
                up[half] = up[half] + gain
                term = (gain + held[level, 2 + half]) * planck_part[half]
                long_sum = term if half == 0 else long_sum + term
                taken = held[level, 4 + half] * sup[half]
                sup[half] = sup[half] - taken + held[level, 6 + half]
                term = (taken + held[level, 8 + half]) * flux[half]
                short_sum = term if half == 0 else short_sum + term
            result = jnp.where(lane == level, jnp.sum(long_sum, axis=1, keepdims=True), result)
            result = jnp.where(
                lane == LEVELS + level, jnp.sum(short_sum, axis=1, keepdims=True), result
            )
        flag = jnp.where(step < PEERS // WIDE, lit[0], lit[1]).astype(jnp.float32)
        is_long = lane < LEVELS
        thickness = jnp.where(is_long, fields, pltpu.roll(fields, LEVELS, 1))
        factor = jnp.where(is_long, -1.0 / 256.0, cosine * (flag / 224.0))
        keep = lane < 2 * LEVELS
        heat[pl.ds(start, WIDE), :] = jnp.where(
            keep, result * factor / jnp.where(keep, thickness, 1.0), 0.0
        )
        return carry

    lax.fori_loop(0, COLS // WIDE, body, 0)


def two(row):
    return [jnp.broadcast_to(row[:, 0:128], (WIDE, 128)), jnp.broadcast_to(row[:, 128:256], (WIDE, 128))]


def short_row(ref, fill):
    row = ref[...]
    return jnp.concatenate([row, jnp.full((1, 32), fill, jnp.float32)], axis=1)


def exchange(count, me, outgoing, incoming, send_sem, recv_sem):
    def copy_to(step):
        peer = lax.rem(me + step, count)
        return pltpu.make_async_remote_copy(
            src_ref=outgoing.at[peer],
            dst_ref=incoming.at[me],
            send_sem=send_sem,
            recv_sem=recv_sem,
            device_id=(peer // 16, lax.rem(peer, 16)),
            device_id_type=pl.DeviceIdType.MESH,
        )

    def start(step, carry):
        copy_to(step).start()
        return carry

    lax.fori_loop(1, count, start, 0)


def await_all(count, outgoing, incoming, send_sem, recv_sem):
    most = count - 1
    pltpu.make_async_copy(
        outgoing.at[pl.ds(0, most)], incoming.at[pl.ds(0, most)], send_sem
    ).wait()
    pltpu.make_async_copy(
        outgoing.at[pl.ds(0, most)], incoming.at[pl.ds(0, most)], recv_sem
    ).wait()


def load_tables(long_hbm, short_hbm, long_in, short_in, sems):
    copies = []
    for piece in range(4):
        part = pl.ds(piece * 1920, min(1920, NTAB - piece * 1920))
        copies.append(
            pltpu.make_async_copy(long_hbm.at[part], long_in.at[part], sems.at[piece])
        )
    for piece in range(2):
        part = pl.ds(piece * 112, 112)
        copies.append(
            pltpu.make_async_copy(short_hbm.at[part], short_in.at[part], sems.at[4 + piece])
        )
    return copies


def column_kernel(
    lit,
    targets,
    amount,
    scatter,
    cloud_path,
    planck,
    thickness,
    cosine,
    albedo,
    surface,
    weights,
    index,
    cloud_long,
    cloud_short,
    planck_part,
    ray,
    flux,
    long_hbm,
    short_hbm,
    long_out,
    short_out,
    table,
    long_in,
    short_in,
    rows_v,
    rows,
    lanes,
    kappa,
    state,
    heat,
    held,
    outgoing,
    incoming,
    back_out,
    back_in,
    sems,
    send_sem,
    recv_sem,
):
    me = lax.axis_index("face") * 16 + lax.axis_index("elem")
    copies = load_tables(long_hbm, short_hbm, long_in, short_in, sems)
    for copy in copies:
        copy.start()
    barrier = pltpu.get_barrier_semaphore()

    def greet(step, carry):
        peer = lax.rem(me + step, PEERS)
        pl.semaphore_signal(
            barrier,
            inc=1,
            device_id=(peer // 16, lax.rem(peer, 16)),
            device_id_type=pl.DeviceIdType.MESH,
        )
        return carry

    lax.fori_loop(1, PEERS, greet, 0)
    rows_v[...] = index[...] * 4
    rows_copy = pltpu.make_async_copy(rows_v, rows, sems.at[6])
    rows_copy.start()

    slot, position = slots_of(targets[pl.ds(2 * me, 2), :])
    fields = jnp.concatenate(
        [
            thickness[...],
            amount[...],
            scatter[...],
            cloud_path[...],
            planck[...],
            as_row(cosine[...]),
            as_row(albedo[...]),
            as_row(surface[...]),
            position,
            jnp.zeros((4, COLS), jnp.float32),
        ],
        axis=0,
    )
    chooser = onehot(slot == iota((COLS, COLS), 0).astype(jnp.float32))
    packed = pick(chooser, fields, 1).reshape(PEERS, 2, 128)
    outgoing[...] = packed
    spread_weights(weights, lanes)
    pl.semaphore_wait(barrier, PEERS - 1)
    exchange(PEERS, me, outgoing, incoming, send_sem.at[0], recv_sem.at[0])
    own = pltpu.make_async_copy(outgoing.at[me], incoming.at[me], sems.at[7])
    own.start()
    for copy in copies:
        copy.wait()
    fill_table(long_in, short_in, table)
    rows_copy.wait()
    gather(rows, table, lanes, kappa)
    own.wait()
    await_all(PEERS, outgoing, incoming, send_sem.at[0], recv_sem.at[0])
    got = incoming[...].reshape(COLS, 128)
    arrived = got[:, 123:124]
    state[...] = pick(onehot(to_row(arrived) == iota((COLS, COLS), 0).astype(jnp.float32)), got)
    params = (
        two(as_row(cloud_long[...]) * 2.0),
        two(as_row(planck_part[...])),
        two(short_row(cloud_short, 0.0)),
        two(short_row(ray, 1.0)),
        two(short_row(flux, 0.0)),
    )
    radiate(state, kappa, heat, lit, params, held)
    back = onehot(arrived == iota((COLS, COLS), 1).astype(jnp.float32))
    back_out[...] = pick(back, heat[...]).reshape(PEERS, 2, 128)
    exchange(PEERS, me, back_out, back_in, send_sem.at[1], recv_sem.at[1])
    own = pltpu.make_async_copy(back_out.at[me], back_in.at[me], sems.at[7])
    own.start()
    own.wait()
    await_all(PEERS, back_out, back_in, send_sem.at[1], recv_sem.at[1])
    home = onehot(to_column(slot) == iota((COLS, COLS), 1).astype(jnp.float32))
    final = pick(home, back_in[...].reshape(COLS, 128)).T
    long_out[...] = final[:LEVELS]
    short_out[...] = final[LEVELS:2 * LEVELS]


def on_device(
    amount,
    scatter,
    cloud_path,
    planck,
    thickness,
    corner_weights,
    table_index,
    cosine,
    albedo,
    surface_source,
    stretch_map,
    sunlit,
    table_longwave,
    table_shortwave,
    cloud_longwave,
    cloud_shortwave,
    planck_fraction,
    rayleigh,
    solar_flux,
):
    anywhere = pl.BlockSpec(memory_space=pl.ANY)
    vector = pl.BlockSpec(memory_space=pltpu.VMEM)
    scalar = pl.BlockSpec(memory_space=pltpu.SMEM)
    field = jax.ShapeDtypeStruct((LEVELS, COLS), jnp.float32)
    buffer = pltpu.VMEM((PEERS, 2, 128), jnp.float32)
    return pl.pallas_call(
        column_kernel,
        out_shape=(field, field),
        in_specs=[scalar] + [vector] * 16 + [anywhere] * 2,
        out_specs=(vector, vector),
        scratch_shapes=[
            pltpu.VMEM((NTAB * 4, 128), jnp.float32),
            pltpu.VMEM((NTAB, 256), jnp.bfloat16),
            pltpu.VMEM((256, NTAB), jnp.bfloat16),
            pltpu.VMEM((LEVELS, COLS), jnp.int32),
            pltpu.SMEM((LEVELS, COLS), jnp.int32),
            pltpu.VMEM((3 * COLS, 256), jnp.float32),
            pltpu.VMEM((3 * COLS * 32, 128), jnp.float32),
            pltpu.VMEM((COLS, 128), jnp.float32),
            pltpu.VMEM((COLS, 128), jnp.float32),
            pltpu.VMEM((LEVELS, 10, WIDE, 128), jnp.float32),
            buffer,
            buffer,
            buffer,
            buffer,
            pltpu.SemaphoreType.DMA((8,)),
            pltpu.SemaphoreType.DMA((2,)),
            pltpu.SemaphoreType.DMA((2,)),
        ],
        compiler_params=pltpu.CompilerParams(
            collective_id=0, has_side_effects=True, vmem_limit_bytes=60 * 2**20
        ),
    )(
        sunlit,
        stretch_map.reshape(COLS, 128),
        amount,
        scatter,
        cloud_path,
        planck,
        thickness,
        cosine.reshape(2, 128),
        albedo.reshape(2, 128),
        surface_source.reshape(2, 128),
        corner_weights,
        table_index,
        cloud_longwave.reshape(2, 128),
        cloud_shortwave.reshape(1, 224),
        planck_fraction.reshape(2, 128),
        rayleigh.reshape(1, 224),
        solar_flux.reshape(1, 224),
        table_longwave,
        table_shortwave.T,
    )


def solution(mesh):
    columns = P(None, ("face", "elem"))
    single = P(("face", "elem"))
    in_specs = (
        (columns,) * 5
        + (P(None, None, ("face", "elem")), columns)
        + (single,) * 3
        + (P(), single)
        + (P(),) * 7
    )
    return jax.shard_map(
        on_device, mesh=mesh, in_specs=in_specs, out_specs=(columns, columns), check_vma=False
    )
```

```python
import functools
import math
import jax
import jax.numpy as jnp
from jax import lax
from jax.experimental import pallas as pl
from jax.experimental.pallas import tpu as pltpu
from jax.sharding import PartitionSpec as P

LEVELS = 24
NT_TEMP = 14
NT_PRES = 60
NTAB = 7560
COLS = 256
FULL = NTAB // 16 * 16
SCALE = -0.83 / math.log(2.0)
CORNERS = tuple(4 * (e * NT_TEMP * NT_PRES + t * NT_PRES) for e in range(2) for t in range(2))
GROUP = 64
PITCH = 40
FACES = 8
ELEMS = 16
WIDE = 16


def iota(shape, axis):
    return lax.broadcasted_iota(jnp.int32, shape, axis)


def parts(x):
    high = x.astype(jnp.bfloat16)
    rest = x - high.astype(jnp.float32)
    middle = rest.astype(jnp.bfloat16)
    low = (rest - middle.astype(jnp.float32)).astype(jnp.bfloat16)
    return (low, middle, high)


def pick(chooser, x, contract=0):
    total = None
    for part in parts(x):
        term = lax.dot_general(
            chooser, part, (((1,), (contract,)), ((), ())), preferred_element_type=jnp.float32
        )
        total = term if total is None else total + term
    return total


def as_row(pair):
    return jnp.concatenate([pair[0:1], pair[1:2]], axis=1)


def eye():
    return iota((COLS, COLS), 0) == iota((COLS, COLS), 1)


def to_column(row):
    return jnp.sum(jnp.where(eye(), row, 0.0), axis=1, keepdims=True)


def to_row(column):
    return jnp.sum(jnp.where(eye(), column, 0.0), axis=0, keepdims=True)


def onehot(mask):
    return jnp.where(mask, 1.0, 0.0).astype(jnp.bfloat16)


def slots_of(targets):
    target_row = as_row(targets)
    owner = (target_row >> 8).astype(jnp.float32)
    position = (target_row & 255).astype(jnp.float32)
    earlier = (to_column(owner) == owner) & (iota((COLS, COLS), 0) < iota((COLS, COLS), 1))
    rank = jnp.sum(jnp.where(earlier, 1.0, 0.0), axis=0, keepdims=True)
    return 2.0 * owner + rank, position


def fill_table(long_in, short_in, table):
    def long_rows(base, count):
        rows = long_in[pl.ds(base, count), :].astype(jnp.float32) * 2.0
        table[pl.ds(base * 4, count, 4), :] = rows[:, :128]
        table[pl.ds(base * 4 + 1, count, 4), :] = rows[:, 128:]

    def long_body(step, carry):
        for inner in range(8):
            long_rows(pl.multiple_of(step * 128, 128) + inner * 16, 16)
        return carry

    lax.fori_loop(0, FULL // 128, long_body, 0)
    long_rows(FULL, NTAB - FULL)

    def short_rows(block, base, count):
        unit = onehot(iota((count, count), 0) == iota((count, count), 1))
        rows = lax.dot_general(
            unit, block, (((1,), (1,)), ((), ())), preferred_element_type=jnp.float32
        )
        table[pl.ds(base * 4 + 2, count, 4), :] = rows[:, :128]
        table[pl.ds(base * 4 + 3, count, 4), :] = rows[:, 128:]

    def short_body(step, carry):
        base = pl.multiple_of(step * 256, 256)
        short_rows(short_in[:, pl.ds(base, 256)], base, 256)
        return carry

    short_in[224:256, :] = jnp.zeros((32, NTAB), jnp.bfloat16)
    lax.fori_loop(0, NTAB // 256, short_body, 0)
    short_rows(short_in[:, FULL - 128:FULL], FULL - 128, 128)
    short_rows(short_in[:, FULL:NTAB], FULL, NTAB - FULL)


def spread_weights(weights, lanes):
    source, lane = iota((64, 256), 0), iota((64, 256), 1)
    expand = onehot((source // 8 == (lane // 4) % 8) & (source % 8 == lane // 32))
    for third in range(3):
        low = weights[:, third * 8:third * 8 + 8, :].reshape(64, COLS).astype(jnp.bfloat16)
        lanes[third * COLS:(third + 1) * COLS, :] = lax.dot_general(
            low, expand, (((0,), (0,)), ((), ())), preferred_element_type=jnp.float32
        )


def gather(rows, table, lanes, kappa):
    out_row, lane = iota((32, 256), 0), iota((32, 256), 1)
    mask = (out_row // 4 == lane // 32) & (out_row % 4 == lane % 4)

    def body(step, carry):
        third = step // (COLS // GROUP)
        origin = third * 8 * COLS + step % (COLS // GROUP) * GROUP
        for member in range(GROUP):
            place = step * GROUP + member
            picked = []
            for level in range(8):
                base = rows[origin + (level * COLS + member)]
                for corner in CORNERS:
                    picked.append(table[pl.ds(base + corner, 8), :])
            right = jnp.concatenate(picked, axis=0).astype(jnp.bfloat16)
            weight = jnp.broadcast_to(lanes[pl.ds(place, 1), :], (32, 256))
            left = jnp.where(mask, weight, 0.0).astype(jnp.bfloat16)
            kappa[pl.ds(pl.multiple_of(place * PITCH, 8), 32), :] = jnp.dot(
                left, right, preferred_element_type=jnp.float32
            )
        return carry

    lax.fori_loop(0, 3 * COLS // GROUP, body, 0)


def radiate(state, kappa, heat, lit, params, held):
    cloud_long, planck_part, cloud_short, ray, flux = params
    lane = iota((WIDE, 128), 1)

    def body(step, carry):
        start = pl.multiple_of(step * WIDE, WIDE)
        fields = state[pl.ds(start, WIDE), :]
        scaled = fields * SCALE

        def wide(x, at):
            return jnp.broadcast_to(x[:, at:at + 1], (WIDE, 128))

        cosine = wide(fields, 120)
        albedo = wide(fields, 121)
        surface = wide(fields, 122)
        path = (1.0 / 0.83) / cosine
        down = [jnp.zeros((WIDE, 128), jnp.float32) for _ in range(2)]
        sdown = [jnp.zeros((WIDE, 128), jnp.float32) for _ in range(2)]
        direct = [jnp.ones((WIDE, 128), jnp.float32) for _ in range(2)]
        for level in range(LEVELS):
            amount = wide(scaled, 24 + level)
            scatter = wide(scaled, 48 + level)
            cloud = wide(scaled, 72 + level)
            planck = wide(fields, 96 + level)
            origin = (level // 8 * COLS + start) * PITCH + level % 8 * 4
            for half in range(2):
                value = kappa[pl.ds(origin + half, WIDE, PITCH), :]
                absorb = 1.0 - jnp.exp2(amount * value + cloud * cloud_long[half])
                gain = absorb * (planck - down[half])
                down[half] = down[half] + gain
                held[level, half] = absorb
                held[level, 2 + half] = gain
            for half in range(2):
                value = kappa[pl.ds(origin + 2 + half, WIDE, PITCH), :]
                absorbed = amount * value
                scattered = scatter * ray[half] + cloud * cloud_short[half]
                extinct = absorbed + scattered
                lost = direct[half] * (1.0 - jnp.exp2(extinct * path))
                direct[half] = direct[half] - lost
                kept = lost * (absorbed / extinct)
                source = 0.5 * (lost - kept)
                close = 1.0 - jnp.exp2(extinct + absorbed)
                taken = close * sdown[half]
                sdown[half] = sdown[half] - taken + source
                held[level, 4 + half] = close
                held[level, 6 + half] = source
                held[level, 8 + half] = taken + kept
        up = [surface, surface]
        sup = [albedo * (direct[half] + sdown[half]) for half in range(2)]
        result = jnp.zeros((WIDE, 128), jnp.float32)
        for level in reversed(range(LEVELS)):
            planck = wide(fields, 96 + level)
            long_sum, short_sum = None, None
            for half in range(2):
                gain = held[level, half] * (planck - up[half])
                up[half] = up[half] + gain
                term = (gain + held[level, 2 + half]) * planck_part[half]
                long_sum = term if half == 0 else long_sum + term
                taken = held[level, 4 + half] * sup[half]
                sup[half] = sup[half] - taken + held[level, 6 + half]
                term = (taken + held[level, 8 + half]) * flux[half]
                short_sum = term if half == 0 else short_sum + term
            result = jnp.where(lane == level, jnp.sum(long_sum, axis=1, keepdims=True), result)
            result = jnp.where(
                lane == LEVELS + level, jnp.sum(short_sum, axis=1, keepdims=True), result
            )
        flag = jnp.where(step < COLS // 2 // WIDE, lit[0], lit[1]).astype(jnp.float32)
        is_long = lane < LEVELS
        thickness = jnp.where(is_long, fields, pltpu.roll(fields, LEVELS, 1))
        factor = jnp.where(is_long, -1.0 / 256.0, cosine * (flag / 224.0))
        keep = lane < 2 * LEVELS
        heat[pl.ds(start, WIDE), :] = jnp.where(
            keep, result * factor / jnp.where(keep, thickness, 1.0), 0.0
        )
        return carry

    lax.fori_loop(0, COLS // WIDE, body, 0)


def two(row):
    return [jnp.broadcast_to(row[:, 0:128], (WIDE, 128)), jnp.broadcast_to(row[:, 128:256], (WIDE, 128))]


def short_row(ref, fill):
    row = ref[...]
    return jnp.concatenate([row, jnp.full((1, 32), fill, jnp.float32)], axis=1)


def exchange(axis, outgoing, incoming, send_sem, recv_sem):
    count = lax.axis_size(axis)
    me = lax.axis_index(axis)
    for step in range(1, count):
        peer = lax.rem(me + step, count)
        pltpu.make_async_remote_copy(
            src_ref=outgoing(peer),
            dst_ref=incoming(me),
            send_sem=send_sem,
            recv_sem=recv_sem,
            device_id={axis: peer},
            device_id_type=pl.DeviceIdType.MESH,
        ).start()


def await_all(axis, buffer, send_sem, recv_sem):
    whole = buffer.at[pl.ds(0, lax.axis_size(axis) - 1)]
    pltpu.make_async_copy(whole, whole, send_sem).wait()
    pltpu.make_async_copy(whole, whole, recv_sem).wait()


def load_tables(long_hbm, short_hbm, long_in, short_in, sems):
    copies = []
    for piece in range(4):
        part = pl.ds(piece * 1920, min(1920, NTAB - piece * 1920))
        copies.append(
            pltpu.make_async_copy(long_hbm.at[part], long_in.at[part], sems.at[piece])
        )
    for piece in range(2):
        part = pl.ds(piece * 112, 112)
        copies.append(
            pltpu.make_async_copy(short_hbm.at[part], short_in.at[part], sems.at[4 + piece])
        )
    return copies


def column_kernel(
    lit,
    targets,
    amount,
    scatter,
    cloud_path,
    planck,
    thickness,
    cosine,
    albedo,
    surface,
    weights,
    index,
    cloud_long,
    cloud_short,
    planck_part,
    ray,
    flux,
    long_hbm,
    short_hbm,
    returned,
    slot_out,
    table,
    long_in,
    short_in,
    rows_v,
    rows,
    lanes,
    kappa,
    state,
    heat,
    held,
    outgoing,
    middle,
    incoming,
    back_out,
    back_middle,
    sems,
    send_sem,
    recv_sem,
):
    me = lax.axis_index("face") * ELEMS + lax.axis_index("elem")
    copies = load_tables(long_hbm, short_hbm, long_in, short_in, sems)
    for copy in copies:
        copy.start()
    face = lax.axis_index("face")
    elem = lax.axis_index("elem")
    barrier = pltpu.get_barrier_semaphore()
    for axis, count in (("face", FACES), ("elem", ELEMS)):
        for step in range(1, count):
            pl.semaphore_signal(
                barrier,
                inc=1,
                device_id={axis: lax.rem(lax.axis_index(axis) + step, count)},
                device_id_type=pl.DeviceIdType.MESH,
            )
    rows_v[...] = index[...] * 4
    row_copies = []
    for level in range(LEVELS):
        row_copies.append(
            pltpu.make_async_copy(rows_v.at[level], rows.at[pl.ds(level * COLS, COLS)], sems.at[6])
        )
    for copy in row_copies:
        copy.start()

    slot, position = slots_of(targets[pl.ds(2 * me, 2), :])
    fields = jnp.concatenate(
        [
            thickness[...],
            amount[...],
            scatter[...],
            cloud_path[...],
            planck[...],
            as_row(cosine[...]),
            as_row(albedo[...]),
            as_row(surface[...]),
            position,
            jnp.zeros((4, COLS), jnp.float32),
        ],
        axis=0,
    )
    chooser = onehot(slot == iota((COLS, COLS), 0).astype(jnp.float32))
    slot_out[...] = slot
    outgoing[...] = pick(chooser, fields, 1).reshape(FACES, ELEMS, 2, 128)
    own = pltpu.make_async_copy(outgoing.at[face], middle.at[face], sems.at[7])
    own.start()
    spread_weights(weights, lanes)
    pl.semaphore_wait(barrier, FACES + ELEMS - 2)
    exchange(
        "face", lambda k: outgoing.at[k], lambda k: middle.at[k], send_sem.at[0], recv_sem.at[0]
    )
    for copy in copies:
        copy.wait()
    fill_table(long_in, short_in, table)
    own.wait()
    await_all("face", middle, send_sem.at[0], recv_sem.at[0])
    exchange(
        "elem", lambda k: middle.at[:, k], lambda k: incoming.at[k], send_sem.at[1], recv_sem.at[1]
    )
    own = pltpu.make_async_copy(middle.at[:, elem], incoming.at[elem], sems.at[7])
    own.start()
    for copy in row_copies:
        copy.wait()
    gather(rows, table, lanes, kappa)
    own.wait()
    await_all("elem", incoming, send_sem.at[1], recv_sem.at[1])
    got = incoming[...].reshape(COLS, 128)
    arrived = got[:, 123:124]
    state[...] = pick(onehot(to_row(arrived) == iota((COLS, COLS), 0).astype(jnp.float32)), got)
    params = (
        two(as_row(cloud_long[...]) * 2.0),
        two(as_row(planck_part[...])),
        two(short_row(cloud_short, 0.0)),
        two(short_row(ray, 1.0)),
        two(short_row(flux, 0.0)),
    )
    radiate(state, kappa, heat, lit, params, held)
    back = onehot(arrived == iota((COLS, COLS), 1).astype(jnp.float32))
    back_out[...] = pick(back, heat[...]).reshape(ELEMS, FACES, 2, 128)
    own = pltpu.make_async_copy(back_out.at[elem], back_middle.at[:, elem], sems.at[7])
    own.start()
    exchange(
        "elem", lambda k: back_out.at[k], lambda k: back_middle.at[:, k], send_sem.at[2], recv_sem.at[2]
    )
    own.wait()
    await_all("elem", back_out, send_sem.at[2], recv_sem.at[2])
    exchange(
        "face", lambda k: back_middle.at[k], lambda k: returned.at[k], send_sem.at[3], recv_sem.at[3]
    )
    own = pltpu.make_async_copy(back_middle.at[face], returned.at[face], sems.at[7])
    own.start()
    own.wait()
    await_all("face", back_middle, send_sem.at[3], recv_sem.at[3])


def home_kernel(returned, slot, long_out, short_out):
    home = onehot(to_column(slot[...]) == iota((COLS, COLS), 1).astype(jnp.float32))
    final = pick(home, returned[...].reshape(COLS, 128)).T
    long_out[...] = final[:LEVELS]
    short_out[...] = final[LEVELS:2 * LEVELS]


def on_device(
    amount,
    scatter,
    cloud_path,
    planck,
    thickness,
    corner_weights,
    table_index,
    cosine,
    albedo,
    surface_source,
    stretch_map,
    sunlit,
    table_longwave,
    table_shortwave,
    cloud_longwave,
    cloud_shortwave,
    planck_fraction,
    rayleigh,
    solar_flux,
):
    anywhere = pl.BlockSpec(memory_space=pl.ANY)
    vector = pl.BlockSpec(memory_space=pltpu.VMEM)
    scalar = pl.BlockSpec(memory_space=pltpu.SMEM)
    field = jax.ShapeDtypeStruct((LEVELS, COLS), jnp.float32)
    by_face = pltpu.VMEM((FACES, ELEMS, 2, 128), jnp.float32)
    by_elem = pltpu.VMEM((ELEMS, FACES, 2, 128), jnp.float32)
    returned, slot = pl.pallas_call(
        column_kernel,
        out_shape=(
            jax.ShapeDtypeStruct((FACES, ELEMS, 2, 128), jnp.float32),
            jax.ShapeDtypeStruct((1, COLS), jnp.float32),
        ),
        in_specs=[scalar] + [vector] * 16 + [anywhere] * 2,
        out_specs=(anywhere, vector),
        scratch_shapes=[
            pltpu.VMEM((NTAB * 4, 128), jnp.float32),
            pltpu.VMEM((NTAB, 256), jnp.bfloat16),
            pltpu.VMEM((256, NTAB), jnp.bfloat16),
            pltpu.VMEM((LEVELS, COLS), jnp.int32),
            pltpu.SMEM((LEVELS * COLS,), jnp.int32),
            pltpu.VMEM((3 * COLS, 256), jnp.float32),
            pltpu.VMEM((3 * COLS * PITCH, 128), jnp.float32),
            pltpu.VMEM((COLS, 128), jnp.float32),
            pltpu.VMEM((COLS, 128), jnp.float32),
            pltpu.VMEM((LEVELS, 10, WIDE, 128), jnp.float32),
            by_face,
            by_face,
            by_elem,
            by_elem,
            by_face,
            pltpu.SemaphoreType.DMA((8,)),
            pltpu.SemaphoreType.DMA((4,)),
            pltpu.SemaphoreType.DMA((4,)),
        ],
        compiler_params=pltpu.CompilerParams(
            collective_id=0, has_side_effects=True, vmem_limit_bytes=60 * 2**20
        ),
    )(
        sunlit,
        stretch_map.reshape(COLS, 128),
        amount,
        scatter,
        cloud_path,
        planck,
        thickness,
        cosine.reshape(2, 128),
        albedo.reshape(2, 128),
        surface_source.reshape(2, 128),
        corner_weights,
        table_index,
        cloud_longwave.reshape(2, 128),
        cloud_shortwave.reshape(1, 224),
        planck_fraction.reshape(2, 128),
        rayleigh.reshape(1, 224),
        solar_flux.reshape(1, 224),
        table_longwave,
        table_shortwave.T,
    )
    return pl.pallas_call(
        home_kernel,
        out_shape=(field, field),
        in_specs=[vector, vector],
        out_specs=(vector, vector),
    )(returned, slot)


def solution(mesh):
    columns = P(None, ("face", "elem"))
    single = P(("face", "elem"))
    in_specs = (
        (columns,) * 5
        + (P(None, None, ("face", "elem")), columns)
        + (single,) * 3
        + (P(), single)
        + (P(),) * 7
    )
    return jax.shard_map(
        on_device, mesh=mesh, in_specs=in_specs, out_specs=(columns, columns), check_vma=False
    )
```

```python
import functools
import math
import jax
import jax.numpy as jnp
from jax import lax
from jax.experimental import pallas as pl
from jax.experimental.pallas import tpu as pltpu
from jax.sharding import PartitionSpec as P

LEVELS = 24
NT_TEMP = 14
NT_PRES = 60
NTAB = 7560
COLS = 256
FULL = NTAB // 16 * 16
SCALE = -0.83 / math.log(2.0)
CORNERS = tuple(4 * (e * NT_TEMP * NT_PRES + t * NT_PRES) for e in range(2) for t in range(2))
GROUP = 64
PITCH = 40
FACES = 8
ELEMS = 16
WIDE = 16


def iota(shape, axis):
    return lax.broadcasted_iota(jnp.int32, shape, axis)


def parts(x):
    high = x.astype(jnp.bfloat16)
    rest = x - high.astype(jnp.float32)
    middle = rest.astype(jnp.bfloat16)
    low = (rest - middle.astype(jnp.float32)).astype(jnp.bfloat16)
    return (low, middle, high)


def pick(chooser, x, contract=0):
    total = None
    for part in parts(x):
        term = lax.dot_general(
            chooser, part, (((1,), (contract,)), ((), ())), preferred_element_type=jnp.float32
        )
        total = term if total is None else total + term
    return total


def as_row(pair):
    return jnp.concatenate([pair[0:1], pair[1:2]], axis=1)


def eye():
    return iota((COLS, COLS), 0) == iota((COLS, COLS), 1)


def to_column(row):
    return jnp.sum(jnp.where(eye(), row, 0.0), axis=1, keepdims=True)


def to_row(column):
    return jnp.sum(jnp.where(eye(), column, 0.0), axis=0, keepdims=True)


def onehot(mask):
    return jnp.where(mask, 1.0, 0.0).astype(jnp.bfloat16)


def slots_of(targets):
    target_row = as_row(targets)
    owner = (target_row >> 8).astype(jnp.float32)
    position = (target_row & 255).astype(jnp.float32)
    earlier = (to_column(owner) == owner) & (iota((COLS, COLS), 0) < iota((COLS, COLS), 1))
    rank = jnp.sum(jnp.where(earlier, 1.0, 0.0), axis=0, keepdims=True)
    return 2.0 * owner + rank, position


def fill_long(long_in, table):
    def rows_at(base, count):
        rows = long_in[pl.ds(base, count), :].astype(jnp.float32) * 2.0
        table[pl.ds(base * 4, count, 4), :] = rows[:, :128]
        table[pl.ds(base * 4 + 1, count, 4), :] = rows[:, 128:]

    def body(step, carry):
        for inner in range(8):
            rows_at(pl.multiple_of(step * 128, 128) + inner * 16, 16)
        return carry

    lax.fori_loop(0, FULL // 128, body, 0)
    rows_at(FULL, NTAB - FULL)


def fill_short(short_in, table):
    def rows_at(block, base, count):
        rows = block.astype(jnp.float32).T
        table[pl.ds(base * 4 + 2, count, 4), :] = rows[:, :128]
        table[pl.ds(base * 4 + 3, count, 4), :] = rows[:, 128:]

    def body(step, carry):
        for inner in range(4):
            base = pl.multiple_of(step * 1024, 256) + inner * 256
            rows_at(short_in[:, pl.ds(base, 256)], base, 256)
        return carry

    short_in[224:256, :] = jnp.zeros((32, NTAB), jnp.bfloat16)
    lax.fori_loop(0, NTAB // 1024, body, 0)
    for base in range(NTAB // 1024 * 1024, FULL, 128):
        rows_at(short_in[:, base:base + 128], base, 128)
    rows_at(short_in[:, FULL:NTAB], FULL, NTAB - FULL)


def spread_weights(weights, lanes):
    source, lane = iota((64, 256), 0), iota((64, 256), 1)
    expand = onehot((source // 8 == (lane // 4) % 8) & (source % 8 == lane // 32))
    for third in range(3):
        low = weights[:, third * 8:third * 8 + 8, :].reshape(64, COLS).astype(jnp.bfloat16)
        lanes[third * COLS:(third + 1) * COLS, :] = lax.dot_general(
            low, expand, (((0,), (0,)), ((), ())), preferred_element_type=jnp.float32
        )


def gather(rows, table, lanes, kappa, first, last):
    out_row, lane = iota((32, 256), 0), iota((32, 256), 1)
    mask = (out_row // 4 == lane // 32) & (out_row % 4 == lane % 4)

    def body(step, carry):
        third = step // (COLS // GROUP)
        origin = third * 8 * COLS + step % (COLS // GROUP) * GROUP
        for member in range(GROUP):
            place = step * GROUP + member
            picked = []
            for level in range(8):
                base = rows[origin + (level * COLS + member)]
                for corner in CORNERS:
                    picked.append(table[pl.ds(base + corner, 8), :])
            right = jnp.concatenate(picked, axis=0).astype(jnp.bfloat16)
            weight = jnp.broadcast_to(lanes[pl.ds(place, 1), :], (32, 256))
            left = jnp.where(mask, weight, 0.0).astype(jnp.bfloat16)
            kappa[pl.ds(pl.multiple_of(place * PITCH, 8), 32), :] = jnp.dot(
                left, right, preferred_element_type=jnp.float32
            )
        return carry

    lax.fori_loop(first, last, body, 0)


def radiate(state, kappa, heat, lit, params, held):
    cloud_long, planck_part, cloud_short, ray, flux = params
    lane = iota((WIDE, 128), 1)

    def body(step, carry):
        start = pl.multiple_of(step * WIDE, WIDE)
        fields = state[pl.ds(start, WIDE), :]
        scaled = fields * SCALE

        def wide(x, at):
            return jnp.broadcast_to(x[:, at:at + 1], (WIDE, 128))

        cosine = wide(fields, 120)
        albedo = wide(fields, 121)
        surface = wide(fields, 122)
        path = (1.0 / 0.83) / cosine
        down = [jnp.zeros((WIDE, 128), jnp.float32) for _ in range(2)]
        sdown = [jnp.zeros((WIDE, 128), jnp.float32) for _ in range(2)]
        direct = [jnp.ones((WIDE, 128), jnp.float32) for _ in range(2)]
        for level in range(LEVELS):
            amount = wide(scaled, 24 + level)
            scatter = wide(scaled, 48 + level)
            cloud = wide(scaled, 72 + level)
            planck = wide(fields, 96 + level)
            origin = (level // 8 * COLS + start) * PITCH + level % 8 * 4
            for half in range(2):
                value = kappa[pl.ds(origin + half, WIDE, PITCH), :]
                absorb = 1.0 - jnp.exp2(amount * value + cloud * cloud_long[half])
                gain = absorb * (planck - down[half])
                down[half] = down[half] + gain
                held[level, half] = absorb
                held[level, 2 + half] = gain
            for half in range(2):
                value = kappa[pl.ds(origin + 2 + half, WIDE, PITCH), :]
                absorbed = amount * value
                scattered = scatter * ray[half] + cloud * cloud_short[half]
                extinct = absorbed + scattered
                lost = direct[half] * (1.0 - jnp.exp2(extinct * path))
                direct[half] = direct[half] - lost
                kept = lost * (absorbed / extinct)
                source = 0.5 * (lost - kept)
                close = 1.0 - jnp.exp2(extinct + absorbed)
                taken = close * sdown[half]
                sdown[half] = sdown[half] - taken + source
                held[level, 4 + half] = close
                held[level, 6 + half] = source
                held[level, 8 + half] = taken + kept
        up = [surface, surface]
        sup = [albedo * (direct[half] + sdown[half]) for half in range(2)]
        result = jnp.zeros((WIDE, 128), jnp.float32)
        for level in reversed(range(LEVELS)):
            planck = wide(fields, 96 + level)
            long_sum, short_sum = None, None
            for half in range(2):
                gain = held[level, half] * (planck - up[half])
                up[half] = up[half] + gain
                term = (gain + held[level, 2 + half]) * planck_part[half]
                long_sum = term if half == 0 else long_sum + term
                taken = held[level, 4 + half] * sup[half]
                sup[half] = sup[half] - taken + held[level, 6 + half]
                term = (taken + held[level, 8 + half]) * flux[half]
                short_sum = term if half == 0 else short_sum + term
            result = jnp.where(lane == level, jnp.sum(long_sum, axis=1, keepdims=True), result)
            result = jnp.where(
                lane == LEVELS + level, jnp.sum(short_sum, axis=1, keepdims=True), result
            )
        flag = jnp.where(step < COLS // 2 // WIDE, lit[0], lit[1]).astype(jnp.float32)
        is_long = lane < LEVELS
        thickness = jnp.where(is_long, fields, pltpu.roll(fields, LEVELS, 1))
        factor = jnp.where(is_long, -1.0 / 256.0, cosine * (flag / 224.0))
        keep = lane < 2 * LEVELS
        heat[pl.ds(start, WIDE), :] = jnp.where(
            keep, result * factor / jnp.where(keep, thickness, 1.0), 0.0
        )
        return carry

    lax.fori_loop(0, COLS // WIDE, body, 0)


def two(row):
    return [jnp.broadcast_to(row[:, 0:128], (WIDE, 128)), jnp.broadcast_to(row[:, 128:256], (WIDE, 128))]


def short_row(ref, fill):
    row = ref[...]
    return jnp.concatenate([row, jnp.full((1, 32), fill, jnp.float32)], axis=1)


def exchange(axis, outgoing, incoming, send_sem, recv_sem):
    count = lax.axis_size(axis)
    me = lax.axis_index(axis)
    for step in range(1, count):
        peer = lax.rem(me + step, count)
        pltpu.make_async_remote_copy(
            src_ref=outgoing(peer),
            dst_ref=incoming(me),
            send_sem=send_sem,
            recv_sem=recv_sem,
            device_id={axis: peer},
            device_id_type=pl.DeviceIdType.MESH,
        ).start()


def await_all(axis, buffer, send_sem, recv_sem):
    whole = buffer.at[pl.ds(0, lax.axis_size(axis) - 1)]
    pltpu.make_async_copy(whole, whole, send_sem).wait()
    pltpu.make_async_copy(whole, whole, recv_sem).wait()


def load_tables(long_hbm, short_hbm, long_in, short_in, sems):
    copies = []
    for piece in range(4):
        part = pl.ds(piece * 1920, min(1920, NTAB - piece * 1920))
        copies.append(
            pltpu.make_async_copy(long_hbm.at[part], long_in.at[part], sems.at[piece])
        )
    for piece in range(2):
        part = pl.ds(piece * 112, 112)
        copies.append(
            pltpu.make_async_copy(short_hbm.at[part], short_in.at[part], sems.at[4 + piece])
        )
    return copies


def column_kernel(
    lit,
    targets,
    amount,
    scatter,
    cloud_path,
    planck,
    thickness,
    cosine,
    albedo,
    surface,
    weights,
    index,
    cloud_long,
    cloud_short,
    planck_part,
    ray,
    flux,
    long_hbm,
    short_hbm,
    returned,
    slot_out,
    table,
    long_in,
    short_in,
    rows_v,
    rows,
    lanes,
    kappa,
    state,
    heat,
    held,
    outgoing,
    middle,
    incoming,
    back_out,
    arrival,
    sems,
    send_sem,
    recv_sem,
):
    me = lax.axis_index("face") * ELEMS + lax.axis_index("elem")
    copies = load_tables(long_hbm, short_hbm, long_in, short_in, sems)
    for copy in copies:
        copy.start()
    face = lax.axis_index("face")
    elem = lax.axis_index("elem")
    barrier = pltpu.get_barrier_semaphore()
    for axis, count in (("face", FACES), ("elem", ELEMS)):
        for step in range(1, count):
            pl.semaphore_signal(
                barrier,
                inc=1,
                device_id={axis: lax.rem(lax.axis_index(axis) + step, count)},
                device_id_type=pl.DeviceIdType.MESH,
            )
    rows_v[...] = index[...] * 4
    row_copies = []
    for level in range(LEVELS):
        row_copies.append(
            pltpu.make_async_copy(rows_v.at[level], rows.at[pl.ds(level * COLS, COLS)], sems.at[6])
        )
    for copy in row_copies:
        copy.start()

    slot, position = slots_of(targets[pl.ds(2 * me, 2), :])
    fields = jnp.concatenate(
        [
            thickness[...],
            amount[...],
            scatter[...],
            cloud_path[...],
            planck[...],
            as_row(cosine[...]),
            as_row(albedo[...]),
            as_row(surface[...]),
            position,
            jnp.zeros((4, COLS), jnp.float32),
        ],
        axis=0,
    )
    chooser = onehot(slot == iota((COLS, COLS), 0).astype(jnp.float32))
    slot_out[...] = slot
    outgoing[...] = pick(chooser, fields, 1).reshape(FACES, ELEMS, 2, 128)
    own = pltpu.make_async_copy(outgoing.at[face], middle.at[face], sems.at[7])
    own.start()
    spread_weights(weights, lanes)
    for copy in copies[:4]:
        copy.wait()
    fill_long(long_in, table)
    pl.semaphore_wait(barrier, FACES + ELEMS - 2)
    exchange(
        "face", lambda k: outgoing.at[k], lambda k: middle.at[k], send_sem.at[0], recv_sem.at[0]
    )
    for copy in copies[4:]:
        copy.wait()
    fill_short(short_in, table)
    for copy in row_copies:
        copy.wait()
    steps = 3 * COLS // GROUP
    gather(rows, table, lanes, kappa, 0, steps // 2)
    own.wait()
    await_all("face", middle, send_sem.at[0], recv_sem.at[0])
    exchange(
        "elem", lambda k: middle.at[:, k], lambda k: incoming.at[k], send_sem.at[1], recv_sem.at[1]
    )
    own = pltpu.make_async_copy(middle.at[:, elem], incoming.at[elem], sems.at[7])
    own.start()
    gather(rows, table, lanes, kappa, steps // 2, steps)
    own.wait()
    await_all("elem", incoming, send_sem.at[1], recv_sem.at[1])
    got = incoming[...].reshape(COLS, 128)
    arrived = got[:, 123:124]
    arrival[...] = got
    state[...] = pick(onehot(to_row(arrived) == iota((COLS, COLS), 0).astype(jnp.float32)), got)
    params = (
        two(as_row(cloud_long[...]) * 2.0),
        two(as_row(planck_part[...])),
        two(short_row(cloud_short, 0.0)),
        two(short_row(ray, 1.0)),
        two(short_row(flux, 0.0)),
    )
    radiate(state, kappa, heat, lit, params, held)
    for rank in range(2):
        there = arrival[pl.ds(rank, COLS // 2, 2), :][:, 123:124]
        back = onehot(there == iota((COLS // 2, COLS), 1).astype(jnp.float32))
        found = pick(back, heat[...])
        both = found if rank == 0 else both + pltpu.roll(found, 64, 1)
    back_out[...] = both.reshape(COLS // 2, 1, 128)
    own = pltpu.make_async_copy(
        back_out.at[elem * FACES + face], returned.at[me], sems.at[7]
    )
    own.start()

    def send_one(step):
        peer = (me + step) & (FACES * ELEMS - 1)
        to_face = peer >> 4
        to_elem = peer & 15
        pltpu.make_async_remote_copy(
            src_ref=back_out.at[to_elem * FACES + to_face],
            dst_ref=returned.at[me],
            send_sem=send_sem.at[2],
            recv_sem=recv_sem.at[2],
            device_id=(to_face, to_elem),
            device_id_type=pl.DeviceIdType.MESH,
        ).start()

    def send_home(group, carry):
        for inner in range(9):
            send_one(group * 9 + inner + 1)
        return carry

    lax.fori_loop(0, 14, send_home, 0)
    send_one(127)
    own.wait()
    most = back_out.at[pl.ds(0, FACES * ELEMS - 1)]
    pltpu.make_async_copy(most, most, send_sem.at[2]).wait()
    pltpu.make_async_copy(most, most, recv_sem.at[2]).wait()


def home_kernel(returned, slot, long_out, short_out):
    place = to_column(slot[...])
    peer = jnp.floor(place * 0.5)
    home = onehot(peer == iota((COLS, COLS // 2), 1).astype(jnp.float32))
    both = pick(home, returned[...].reshape(COLS // 2, 128))
    final = jnp.where(place > 2.0 * peer, pltpu.roll(both, 64, 1), both).T
    long_out[...] = final[:LEVELS]
    short_out[...] = final[LEVELS:2 * LEVELS]


def on_device(
    amount,
    scatter,
    cloud_path,
    planck,
    thickness,
    corner_weights,
    table_index,
    cosine,
    albedo,
    surface_source,
    stretch_map,
    sunlit,
    table_longwave,
    table_shortwave,
    cloud_longwave,
    cloud_shortwave,
    planck_fraction,
    rayleigh,
    solar_flux,
):
    anywhere = pl.BlockSpec(memory_space=pl.ANY)
    vector = pl.BlockSpec(memory_space=pltpu.VMEM)
    scalar = pl.BlockSpec(memory_space=pltpu.SMEM)
    field = jax.ShapeDtypeStruct((LEVELS, COLS), jnp.float32)
    by_face = pltpu.VMEM((FACES, ELEMS, 2, 128), jnp.float32)
    by_elem = pltpu.VMEM((ELEMS, FACES, 2, 128), jnp.float32)
    returned, slot = pl.pallas_call(
        column_kernel,
        out_shape=(
            jax.ShapeDtypeStruct((COLS // 2, 1, 128), jnp.float32),
            jax.ShapeDtypeStruct((1, COLS), jnp.float32),
        ),
        in_specs=[scalar] + [vector] * 16 + [anywhere] * 2,
        out_specs=(anywhere, vector),
        scratch_shapes=[
            pltpu.VMEM((NTAB * 4, 128), jnp.float32),
            pltpu.VMEM((NTAB, 256), jnp.bfloat16),
            pltpu.VMEM((256, NTAB), jnp.bfloat16),
            pltpu.VMEM((LEVELS, COLS), jnp.int32),
            pltpu.SMEM((LEVELS * COLS,), jnp.int32),
            pltpu.VMEM((3 * COLS, 256), jnp.float32),
            pltpu.VMEM((3 * COLS * PITCH, 128), jnp.float32),
            pltpu.VMEM((COLS, 128), jnp.float32),
            pltpu.VMEM((COLS, 128), jnp.float32),
            pltpu.VMEM((LEVELS, 10, WIDE, 128), jnp.float32),
            by_face,
            by_face,
            by_elem,
            pltpu.VMEM((COLS // 2, 1, 128), jnp.float32),
            pltpu.VMEM((COLS, 128), jnp.float32),
            pltpu.SemaphoreType.DMA((8,)),
            pltpu.SemaphoreType.DMA((3,)),
            pltpu.SemaphoreType.DMA((3,)),
        ],
        compiler_params=pltpu.CompilerParams(
            collective_id=0, has_side_effects=True, vmem_limit_bytes=60 * 2**20
        ),
    )(
        sunlit,
        stretch_map.reshape(COLS, 128),
        amount,
        scatter,
        cloud_path,
        planck,
        thickness,
        cosine.reshape(2, 128),
        albedo.reshape(2, 128),
        surface_source.reshape(2, 128),
        corner_weights,
        table_index,
        cloud_longwave.reshape(2, 128),
        cloud_shortwave.reshape(1, 224),
        planck_fraction.reshape(2, 128),
        rayleigh.reshape(1, 224),
        solar_flux.reshape(1, 224),
        table_longwave,
        table_shortwave.T,
    )
    return pl.pallas_call(
        home_kernel,
        out_shape=(field, field),
        in_specs=[vector, vector],
        out_specs=(vector, vector),
    )(returned, slot)


def solution(mesh):
    columns = P(None, ("face", "elem"))
    single = P(("face", "elem"))
    in_specs = (
        (columns,) * 5
        + (P(None, None, ("face", "elem")), columns)
        + (single,) * 3
        + (P(), single)
        + (P(),) * 7
    )
    return jax.shard_map(
        on_device, mesh=mesh, in_specs=in_specs, out_specs=(columns, columns), check_vma=False
    )
```

```python
import functools
import math
import jax
import jax.numpy as jnp
from jax import lax
from jax.experimental import pallas as pl
from jax.experimental.pallas import tpu as pltpu
from jax.sharding import PartitionSpec as P

LEVELS = 24
NT_TEMP = 14
NT_PRES = 60
NTAB = 7560
COLS = 256
FULL = NTAB // 16 * 16
SCALE = -1.66 / math.log(2.0)
SHORT_AT = 32
CORNERS = tuple(4 * (e * NT_TEMP * NT_PRES + t * NT_PRES) for e in range(2) for t in range(2))
GROUP = 128
PITCH = 8
FACES = 8
ELEMS = 16
WIDE = 32


def iota(shape, axis):
    return lax.broadcasted_iota(jnp.int32, shape, axis)


def parts(x):
    high = x.astype(jnp.bfloat16)
    rest = x - high.astype(jnp.float32)
    middle = rest.astype(jnp.bfloat16)
    low = (rest - middle.astype(jnp.float32)).astype(jnp.bfloat16)
    return (low, middle, high)


def pick(chooser, x, contract=0):
    total = None
    for part in parts(x):
        term = lax.dot_general(
            chooser, part, (((1,), (contract,)), ((), ())), preferred_element_type=jnp.float32
        )
        total = term if total is None else total + term
    return total


def as_row(pair):
    return jnp.concatenate([pair[0:1], pair[1:2]], axis=1)


def eye():
    return iota((COLS, COLS), 0) == iota((COLS, COLS), 1)


def to_column(row):
    return jnp.sum(jnp.where(eye(), row, 0.0), axis=1, keepdims=True)


def to_row(column):
    return jnp.sum(jnp.where(eye(), column, 0.0), axis=0, keepdims=True)


def onehot(mask):
    return jnp.where(mask, 1.0, 0.0).astype(jnp.bfloat16)


def slots_of(targets):
    target_row = as_row(targets)
    owner = (target_row >> 8).astype(jnp.float32)
    position = (target_row & 255).astype(jnp.float32)
    earlier = (to_column(owner) == owner) & (iota((COLS, COLS), 0) < iota((COLS, COLS), 1))
    rank = jnp.sum(jnp.where(earlier, 1.0, 0.0), axis=0, keepdims=True)
    return 2.0 * owner + rank, position


def fill_long(long_in, table):
    def rows_at(base, count):
        rows = long_in[pl.ds(base, count), :].astype(jnp.float32)
        table[pl.ds(base * 4, count, 4), :] = rows[:, :128]
        table[pl.ds(base * 4 + 1, count, 4), :] = rows[:, 128:]

    def body(step, carry):
        for inner in range(8):
            rows_at(pl.multiple_of(step * 128, 128) + inner * 16, 16)
        return carry

    lax.fori_loop(0, FULL // 128, body, 0)
    rows_at(FULL, NTAB - FULL)


def fill_short(short_in, table):
    def rows_at(block, base, count):
        rows = block.astype(jnp.float32).T
        table[pl.ds(base * 4 + 2, count, 4), :] = rows[:, :128]
        table[pl.ds(base * 4 + 3, count, 4), :] = rows[:, 128:]

    def body(step, carry):
        for inner in range(4):
            base = pl.multiple_of(step * 1024, 256) + inner * 256
            rows_at(short_in[:, pl.ds(base, 256)], base, 256)
        return carry

    short_in[224:256, :] = jnp.zeros((32, NTAB), jnp.bfloat16)
    lax.fori_loop(0, NTAB // 1024, body, 0)
    for base in range(NTAB // 1024 * 1024, FULL, 128):
        rows_at(short_in[:, base:base + 128], base, 128)
    rows_at(short_in[:, FULL:NTAB], FULL, NTAB - FULL)


def spread_weights(weights, lanes):
    source, lane = iota((64, 256), 0), iota((64, 256), 1)
    expand = onehot((source // 8 == (lane // 4) % 8) & (source % 8 == lane // 32))
    for third in range(3):
        low = weights[:, third * 8:third * 8 + 8, :].reshape(64, COLS).astype(jnp.bfloat16)
        spread = lax.dot_general(
            low, expand, (((0,), (0,)), ((), ())), preferred_element_type=jnp.float32
        )
        for half in range(2):
            lanes[half, third * COLS:(third + 1) * COLS, :] = spread[:, half * 128:half * 128 + 128]


def gather(rows, table, lanes, kappa, first, last):
    out_row, lane = iota((32, 128), 0), iota((32, 128), 1)
    mask = [
        (out_row // 4 == lane // 32 + 4 * half) & (out_row % 4 == lane % 4) for half in range(2)
    ]

    def body(step, carry):
        third = step // (COLS // GROUP)
        first = step % (COLS // GROUP) * GROUP
        origin = third * 8 * COLS + first
        for member in range(GROUP):
            picked = []
            for level in range(8):
                base = rows[origin + (level * COLS + member)]
                for corner in CORNERS:
                    picked.append(table[pl.ds(base + corner, 8), :])
            right = jnp.concatenate(picked, axis=0).astype(jnp.bfloat16)
            row = pl.ds(pl.multiple_of(step * GROUP, GROUP) + member, 1)
            left = jnp.concatenate(
                [
                    jnp.where(mask[half], jnp.broadcast_to(lanes[half, row, :], (32, 128)), 0.0)
                    for half in range(2)
                ],
                axis=1,
            ).astype(jnp.bfloat16)
            found = jnp.dot(left, right, preferred_element_type=jnp.float32)
            for pair in range(4):
                spot = ((third * 4 + pair) * COLS + first + member) * PITCH
                kappa[pl.ds(pl.multiple_of(spot, 8), 8), :] = found[pair * 8:pair * 8 + 8]
        return carry

    lax.fori_loop(first, last, body, 0)


def radiate(state, kappa, heat, lit, params, held):
    cloud_long, planck_part, cloud_short, ray, flux = params
    lane = iota((WIDE, 128), 1)

    def body(step, carry):
        start = pl.multiple_of(step * WIDE, WIDE)
        fields = state[pl.ds(start, WIDE), :]
        scaled = fields * SCALE

        def wide(x, at):
            return jnp.broadcast_to(x[:, at:at + 1], (WIDE, 128))

        cosine = wide(fields, 120)
        albedo = wide(fields, 121)
        surface = wide(fields, 122)
        path = (1.0 / 1.66) / cosine
        down = [jnp.zeros((WIDE, 128), jnp.float32) for _ in range(2)]
        sdown = [jnp.zeros((WIDE, 128), jnp.float32) for _ in range(2)]
        direct = [jnp.ones((WIDE, 128), jnp.float32) for _ in range(2)]
        for level in range(LEVELS):
            amount = wide(scaled, 24 + level)
            scatter = wide(scaled, 48 + level)
            cloud = wide(scaled, 72 + level)
            planck = wide(fields, 96 + level)
            origin = (level // 2 * COLS + start) * PITCH + level % 2 * 4
            for half in range(2):
                value = kappa[pl.ds(origin + half, WIDE, PITCH), :]
                transmit = jnp.exp2(amount * value + cloud * cloud_long[half])
                held[level, half] = transmit
                held[level, 2 + half] = down[half]
                down[half] = planck + transmit * (down[half] - planck)
            for half in range(2):
                value = kappa[pl.ds(origin + 2 + half, WIDE, PITCH), :]
                absorbed = amount * value
                scattered = scatter * ray[half] + cloud * cloud_short[half]
                partial = absorbed + scattered
                extinct = partial + scattered
                onward = direct[half] * jnp.exp2(extinct * path)
                source = (direct[half] - onward) * (scattered / extinct)
                spread = jnp.exp2(partial)
                held[level, 4 + half] = spread
                held[level, 6 + half] = source
                held[level, 8 + half] = direct[half] + sdown[half]
                direct[half] = onward
                sdown[half] = spread * sdown[half] + source
        up = [surface, surface]
        below = [direct[half] + sdown[half] for half in range(2)]
        sup = [albedo * below[half] for half in range(2)]
        result = jnp.zeros((WIDE, 128), jnp.float32)

        def settle(result, face, upper, shorter):
            long_net = [(up[half] - upper[half]) * planck_part[half] for half in range(2)]
            short_net = [(sup[half] - shorter[half]) * flux[half] for half in range(2)]
            long_sum = jnp.sum(long_net[0] + long_net[1], axis=1, keepdims=True)
            short_sum = jnp.sum(short_net[0] + short_net[1], axis=1, keepdims=True)
            result = jnp.where(lane == face, long_sum, result)
            return jnp.where(lane == SHORT_AT + face, short_sum, result)

        result = settle(result, LEVELS, down, below)
        for level in reversed(range(LEVELS)):
            planck = wide(fields, 96 + level)
            for half in range(2):
                up[half] = planck + held[level, half] * (up[half] - planck)
                sup[half] = held[level, 4 + half] * sup[half] + held[level, 6 + half]
            result = settle(
                result,
                level,
                [held[level, 2 + half] for half in range(2)],
                [held[level, 8 + half] for half in range(2)],
            )
        result = pltpu.roll(result, 127, 1) - result
        flag = jnp.where(step < COLS // 2 // WIDE, lit[0], lit[1]).astype(jnp.float32)
        is_long = lane < SHORT_AT
        thickness = jnp.where(is_long, fields, pltpu.roll(fields, SHORT_AT, 1))
        factor = jnp.where(is_long, 1.0 / 256.0, cosine * (flag / 224.0))
        keep = (lane % SHORT_AT < LEVELS) & (lane < 2 * SHORT_AT)
        heat[pl.ds(start, WIDE), :] = jnp.where(
            keep, result * factor / jnp.where(keep, thickness, 1.0), 0.0
        )
        return carry

    lax.fori_loop(0, COLS // WIDE, body, 0)


def two(row):
    return [jnp.broadcast_to(row[:, 0:128], (WIDE, 128)), jnp.broadcast_to(row[:, 128:256], (WIDE, 128))]


def short_row(ref, fill):
    row = ref[...]
    return jnp.concatenate([row, jnp.full((1, 32), fill, jnp.float32)], axis=1)


def exchange(axis, outgoing, incoming, send_sem, recv_sem):
    count = lax.axis_size(axis)
    me = lax.axis_index(axis)
    for step in range(1, count):
        peer = lax.rem(me + step, count)
        pltpu.make_async_remote_copy(
            src_ref=outgoing(peer),
            dst_ref=incoming(me),
            send_sem=send_sem,
            recv_sem=recv_sem,
            device_id={axis: peer},
            device_id_type=pl.DeviceIdType.MESH,
        ).start()


def await_all(axis, buffer, send_sem, recv_sem):
    whole = buffer.at[pl.ds(0, lax.axis_size(axis) - 1)]
    pltpu.make_async_copy(whole, whole, send_sem).wait()
    pltpu.make_async_copy(whole, whole, recv_sem).wait()


def load_tables(long_hbm, short_hbm, long_in, short_in, sems):
    copies = []
    for piece in range(4):
        part = pl.ds(piece * 1920, min(1920, NTAB - piece * 1920))
        copies.append(
            pltpu.make_async_copy(long_hbm.at[part], long_in.at[part], sems.at[piece])
        )
    for piece in range(2):
        part = pl.ds(piece * 112, 112)
        copies.append(
            pltpu.make_async_copy(short_hbm.at[part], short_in.at[part], sems.at[4 + piece])
        )
    return copies


def column_kernel(
    lit,
    targets,
    amount,
    scatter,
    cloud_path,
    planck,
    thickness,
    cosine,
    albedo,
    surface,
    weights,
    index,
    cloud_long,
    cloud_short,
    planck_part,
    ray,
    flux,
    long_hbm,
    short_hbm,
    returned,
    slot_out,
    table,
    long_in,
    short_in,
    rows_v,
    rows,
    lanes,
    kappa,
    state,
    heat,
    held,
    outgoing,
    middle,
    incoming,
    back_out,
    arrival,
    sems,
    send_sem,
    recv_sem,
):
    me = lax.axis_index("face") * ELEMS + lax.axis_index("elem")
    copies = load_tables(long_hbm, short_hbm, long_in, short_in, sems)
    for copy in copies:
        copy.start()
    face = lax.axis_index("face")
    elem = lax.axis_index("elem")
    barrier = pltpu.get_barrier_semaphore()
    for axis, count in (("face", FACES), ("elem", ELEMS)):
        for step in range(1, count):
            pl.semaphore_signal(
                barrier,
                inc=1,
                device_id={axis: lax.rem(lax.axis_index(axis) + step, count)},
                device_id_type=pl.DeviceIdType.MESH,
            )
    rows_v[...] = index[...] * 4
    row_copies = []
    for level in range(LEVELS):
        row_copies.append(
            pltpu.make_async_copy(rows_v.at[level], rows.at[pl.ds(level * COLS, COLS)], sems.at[6])
        )
    for copy in row_copies:
        copy.start()

    slot, position = slots_of(targets[pl.ds(2 * me, 2), :])
    fields = jnp.concatenate(
        [
            thickness[...],
            amount[...],
            scatter[...],
            cloud_path[...],
            planck[...],
            as_row(cosine[...]),
            as_row(albedo[...]),
            as_row(surface[...]),
            position,
            jnp.zeros((4, COLS), jnp.float32),
        ],
        axis=0,
    )
    chooser = onehot(slot == iota((COLS, COLS), 0).astype(jnp.float32))
    slot_out[...] = slot
    outgoing[...] = pick(chooser, fields, 1).reshape(FACES, ELEMS, 2, 128)
    own = pltpu.make_async_copy(outgoing.at[face], middle.at[face], sems.at[7])
    own.start()
    spread_weights(weights, lanes)
    for copy in copies[:4]:
        copy.wait()
    fill_long(long_in, table)
    pl.semaphore_wait(barrier, FACES + ELEMS - 2)
    exchange(
        "face", lambda k: outgoing.at[k], lambda k: middle.at[k], send_sem.at[0], recv_sem.at[0]
    )
    for copy in copies[4:]:
        copy.wait()
    fill_short(short_in, table)
    for copy in row_copies:
        copy.wait()
    steps = 3 * COLS // GROUP
    gather(rows, table, lanes, kappa, 0, steps // 2)
    own.wait()
    await_all("face", middle, send_sem.at[0], recv_sem.at[0])
    exchange(
        "elem", lambda k: middle.at[:, k], lambda k: incoming.at[k], send_sem.at[1], recv_sem.at[1]
    )
    own = pltpu.make_async_copy(middle.at[:, elem], incoming.at[elem], sems.at[7])
    own.start()
    gather(rows, table, lanes, kappa, steps // 2, steps)
    own.wait()
    await_all("elem", incoming, send_sem.at[1], recv_sem.at[1])
    got = incoming[...].reshape(COLS, 128)
    arrived = got[:, 123:124]
    arrival[...] = got
    state[...] = pick(onehot(to_row(arrived) == iota((COLS, COLS), 0).astype(jnp.float32)), got)
    params = (
        two(as_row(cloud_long[...])),
        two(as_row(planck_part[...])),
        two(short_row(cloud_short, 0.0) * 0.5),
        two(short_row(ray, 1.0) * 0.5),
        two(short_row(flux, 0.0)),
    )
    radiate(state, kappa, heat, lit, params, held)
    for rank in range(2):
        there = arrival[pl.ds(rank, COLS // 2, 2), :][:, 123:124]
        back = onehot(there == iota((COLS // 2, COLS), 1).astype(jnp.float32))
        found = pick(back, heat[...])
        both = found if rank == 0 else both + pltpu.roll(found, 64, 1)
    back_out[...] = both.reshape(COLS // 2, 1, 128)
    own = pltpu.make_async_copy(
        back_out.at[elem * FACES + face], returned.at[me], sems.at[7]
    )
    own.start()

    def send_one(step):
        peer = (me + step) & (FACES * ELEMS - 1)
        to_face = peer >> 4
        to_elem = peer & 15
        pltpu.make_async_remote_copy(
            src_ref=back_out.at[to_elem * FACES + to_face],
            dst_ref=returned.at[me],
            send_sem=send_sem.at[2],
            recv_sem=recv_sem.at[2],
            device_id=(to_face, to_elem),
            device_id_type=pl.DeviceIdType.MESH,
        ).start()

    def send_home(group, carry):
        for inner in range(9):
            send_one(group * 9 + inner + 1)
        return carry

    lax.fori_loop(0, 14, send_home, 0)
    send_one(127)
    own.wait()
    most = back_out.at[pl.ds(0, FACES * ELEMS - 1)]
    pltpu.make_async_copy(most, most, send_sem.at[2]).wait()
    pltpu.make_async_copy(most, most, recv_sem.at[2]).wait()


def home_kernel(returned, slot, long_out, short_out):
    place = to_column(slot[...])
    peer = jnp.floor(place * 0.5)
    home = onehot(peer == iota((COLS, COLS // 2), 1).astype(jnp.float32))
    both = pick(home, returned[...].reshape(COLS // 2, 128))
    final = jnp.where(place > 2.0 * peer, pltpu.roll(both, 64, 1), both).T
    long_out[...] = final[:LEVELS]
    short_out[...] = final[SHORT_AT:SHORT_AT + LEVELS]


def on_device(
    amount,
    scatter,
    cloud_path,
    planck,
    thickness,
    corner_weights,
    table_index,
    cosine,
    albedo,
    surface_source,
    stretch_map,
    sunlit,
    table_longwave,
    table_shortwave,
    cloud_longwave,
    cloud_shortwave,
    planck_fraction,
    rayleigh,
    solar_flux,
):
    anywhere = pl.BlockSpec(memory_space=pl.ANY)
    vector = pl.BlockSpec(memory_space=pltpu.VMEM)
    scalar = pl.BlockSpec(memory_space=pltpu.SMEM)
    field = jax.ShapeDtypeStruct((LEVELS, COLS), jnp.float32)
    by_face = pltpu.VMEM((FACES, ELEMS, 2, 128), jnp.float32)
    by_elem = pltpu.VMEM((ELEMS, FACES, 2, 128), jnp.float32)
    returned, slot = pl.pallas_call(
        column_kernel,
        out_shape=(
            jax.ShapeDtypeStruct((COLS // 2, 1, 128), jnp.float32),
            jax.ShapeDtypeStruct((1, COLS), jnp.float32),
        ),
        in_specs=[scalar] + [vector] * 16 + [anywhere] * 2,
        out_specs=(anywhere, vector),
        scratch_shapes=[
            pltpu.VMEM((NTAB * 4, 128), jnp.float32),
            pltpu.VMEM((NTAB, 256), jnp.bfloat16),
            pltpu.VMEM((256, NTAB), jnp.bfloat16),
            pltpu.VMEM((LEVELS, COLS), jnp.int32),
            pltpu.SMEM((LEVELS * COLS,), jnp.int32),
            pltpu.VMEM((2, 3 * COLS, 128), jnp.float32),
            pltpu.VMEM((12 * COLS * PITCH, 128), jnp.float32),
            pltpu.VMEM((COLS, 128), jnp.float32),
            pltpu.VMEM((COLS, 128), jnp.float32),
            pltpu.VMEM((LEVELS, 10, WIDE, 128), jnp.float32),
            by_face,
            by_face,
            by_elem,
            pltpu.VMEM((COLS // 2, 1, 128), jnp.float32),
            pltpu.VMEM((COLS, 128), jnp.float32),
            pltpu.SemaphoreType.DMA((8,)),
            pltpu.SemaphoreType.DMA((3,)),
            pltpu.SemaphoreType.DMA((3,)),
        ],
        compiler_params=pltpu.CompilerParams(
            collective_id=0, has_side_effects=True, vmem_limit_bytes=60 * 2**20
        ),
    )(
        sunlit,
        stretch_map.reshape(COLS, 128),
        amount,
        scatter,
        cloud_path,
        planck,
        thickness,
        cosine.reshape(2, 128),
        albedo.reshape(2, 128),
        surface_source.reshape(2, 128),
        corner_weights,
        table_index,
        cloud_longwave.reshape(2, 128),
        cloud_shortwave.reshape(1, 224),
        planck_fraction.reshape(2, 128),
        rayleigh.reshape(1, 224),
        solar_flux.reshape(1, 224),
        table_longwave,
        table_shortwave.T,
    )
    return pl.pallas_call(
        home_kernel,
        out_shape=(field, field),
        in_specs=[vector, vector],
        out_specs=(vector, vector),
    )(returned, slot)


def solution(mesh):
    columns = P(None, ("face", "elem"))
    single = P(("face", "elem"))
    in_specs = (
        (columns,) * 5
        + (P(None, None, ("face", "elem")), columns)
        + (single,) * 3
        + (P(), single)
        + (P(),) * 7
    )
    return jax.shard_map(
        on_device, mesh=mesh, in_specs=in_specs, out_specs=(columns, columns), check_vma=False
    )
```

```python
import functools
import math
import jax
import jax.numpy as jnp
from jax import lax
from jax.experimental import pallas as pl
from jax.experimental.pallas import tpu as pltpu
from jax.sharding import PartitionSpec as P

LEVELS = 24
NT_TEMP = 14
NT_PRES = 60
NTAB = 7560
COLS = 256
FULL = NTAB // 16 * 16
SCALE = -1.66 / math.log(2.0)
SHORT_AT = 32
CORNERS = tuple(4 * (e * NT_TEMP * NT_PRES + t * NT_PRES) for e in range(2) for t in range(2))
GROUP = 128
PITCH = 8
FACES = 8
ELEMS = 16
WIDE = 32


def iota(shape, axis):
    return lax.broadcasted_iota(jnp.int32, shape, axis)


def parts(x):
    high = x.astype(jnp.bfloat16)
    rest = x - high.astype(jnp.float32)
    middle = rest.astype(jnp.bfloat16)
    low = (rest - middle.astype(jnp.float32)).astype(jnp.bfloat16)
    return (low, middle, high)


def pick(chooser, x, contract=0):
    total = None
    for part in parts(x):
        term = lax.dot_general(
            chooser, part, (((1,), (contract,)), ((), ())), preferred_element_type=jnp.float32
        )
        total = term if total is None else total + term
    return total


def as_row(pair):
    return jnp.concatenate([pair[0:1], pair[1:2]], axis=1)


def eye():
    return iota((COLS, COLS), 0) == iota((COLS, COLS), 1)


def to_column(row):
    return jnp.sum(jnp.where(eye(), row, 0.0), axis=1, keepdims=True)


def to_row(column):
    return jnp.sum(jnp.where(eye(), column, 0.0), axis=0, keepdims=True)


def onehot(mask):
    return jnp.where(mask, 1.0, 0.0).astype(jnp.bfloat16)


def slots_of(targets):
    target_row = as_row(targets)
    owner = (target_row >> 8).astype(jnp.float32)
    position = (target_row & 255).astype(jnp.float32)
    earlier = (to_column(owner) == owner) & (iota((COLS, COLS), 0) < iota((COLS, COLS), 1))
    rank = jnp.sum(jnp.where(earlier, 1.0, 0.0), axis=0, keepdims=True)
    return 2.0 * owner + rank, position


def fill_long(long_in, table):
    def rows_at(base, count):
        rows = long_in[pl.ds(base, count), :].astype(jnp.float32)
        table[pl.ds(base * 4, count, 4), :] = rows[:, :128]
        table[pl.ds(base * 4 + 1, count, 4), :] = rows[:, 128:]

    def body(step, carry):
        for inner in range(8):
            rows_at(pl.multiple_of(step * 128, 128) + inner * 16, 16)
        return carry

    lax.fori_loop(0, FULL // 128, body, 0)
    rows_at(FULL, NTAB - FULL)


def fill_short(short_in, table):
    def rows_at(block, base, count):
        rows = block.astype(jnp.float32).T
        table[pl.ds(base * 4 + 2, count, 4), :] = rows[:, :128]
        table[pl.ds(base * 4 + 3, count, 4), :] = rows[:, 128:]

    def body(step, carry):
        for inner in range(4):
            base = pl.multiple_of(step * 1024, 256) + inner * 256
            rows_at(short_in[:, pl.ds(base, 256)], base, 256)
        return carry

    short_in[224:256, :] = jnp.zeros((32, NTAB), jnp.bfloat16)
    lax.fori_loop(0, NTAB // 1024, body, 0)
    for base in range(NTAB // 1024 * 1024, FULL, 128):
        rows_at(short_in[:, base:base + 128], base, 128)
    rows_at(short_in[:, FULL:NTAB], FULL, NTAB - FULL)


def spread_weights(weights, lanes):
    source, lane = iota((64, 256), 0), iota((64, 256), 1)
    expand = onehot((source // 8 == (lane // 4) % 8) & (source % 8 == lane // 32))
    for third in range(3):
        low = weights[:, third * 8:third * 8 + 8, :].reshape(64, COLS).astype(jnp.bfloat16)
        spread = lax.dot_general(
            low, expand, (((0,), (0,)), ((), ())), preferred_element_type=jnp.float32
        )
        for half in range(2):
            lanes[half, third * COLS:(third + 1) * COLS, :] = spread[:, half * 128:half * 128 + 128]


def gather(rows, table, lanes, kappa, first, last):
    out_row, lane = iota((32, 128), 0), iota((32, 128), 1)
    mask = [
        (out_row // 4 == lane // 32 + 4 * half) & (out_row % 4 == lane % 4) for half in range(2)
    ]

    def body(step, carry):
        third = step // (COLS // GROUP)
        first = step % (COLS // GROUP) * GROUP
        origin = third * 8 * COLS + first
        for member in range(GROUP):
            picked = []
            for level in range(8):
                base = rows[origin + (level * COLS + member)]
                for corner in CORNERS:
                    picked.append(table[pl.ds(base + corner, 8), :])
            right = jnp.concatenate(picked, axis=0).astype(jnp.bfloat16)
            row = pl.ds(pl.multiple_of(step * GROUP, GROUP) + member, 1)
            left = jnp.concatenate(
                [
                    jnp.where(mask[half], jnp.broadcast_to(lanes[half, row, :], (32, 128)), 0.0)
                    for half in range(2)
                ],
                axis=1,
            ).astype(jnp.bfloat16)
            found = jnp.dot(left, right, preferred_element_type=jnp.float32)
            for pair in range(4):
                spot = ((third * 4 + pair) * COLS + first + member) * PITCH
                kappa[pl.ds(pl.multiple_of(spot, 8), 8), :] = found[pair * 8:pair * 8 + 8]
        return carry

    lax.fori_loop(first, last, body, 0)


def radiate(state, kappa, heat, lit, params, held):
    cloud_long, planck_part, cloud_short, ray, flux = params
    lane = iota((WIDE, 128), 1)

    def body(step, carry):
        start = pl.multiple_of(step * WIDE, WIDE)
        fields = state[pl.ds(start, WIDE), :]
        scaled = fields * SCALE

        def wide(x, at):
            return jnp.broadcast_to(x[:, at:at + 1], (WIDE, 128))

        cosine = wide(fields, 120)
        albedo = wide(fields, 121)
        surface = wide(fields, 122)
        path = (1.0 / 1.66) / cosine
        down = [jnp.zeros((WIDE, 128), jnp.float32) for _ in range(2)]
        sdown = [jnp.zeros((WIDE, 128), jnp.float32) for _ in range(2)]
        direct = list(flux)
        for level in range(LEVELS):
            amount = wide(scaled, 24 + level)
            scatter = wide(scaled, 48 + level)
            cloud = wide(scaled, 72 + level)
            planck = wide(fields, 96 + level)
            origin = (level // 2 * COLS + start) * PITCH + level % 2 * 4
            for half in range(2):
                value = kappa[pl.ds(origin + half, WIDE, PITCH), :]
                transmit = jnp.exp2(amount * value + cloud * cloud_long[half])
                held[level, half] = transmit
                held[level, 2 + half] = down[half]
                down[half] = planck + transmit * (down[half] - planck)
            for half in range(2):
                value = kappa[pl.ds(origin + 2 + half, WIDE, PITCH), :]
                absorbed = amount * value
                scattered = scatter * ray[half] + cloud * cloud_short[half]
                partial = absorbed + scattered
                extinct = partial + scattered
                onward = direct[half] * jnp.exp2(extinct * path)
                source = (direct[half] - onward) * (scattered / extinct)
                spread = jnp.exp2(partial)
                held[level, 4 + half] = spread
                held[level, 6 + half] = source
                held[level, 8 + half] = direct[half] + sdown[half]
                direct[half] = onward
                sdown[half] = spread * sdown[half] + source
        up = [surface, surface]
        below = [direct[half] + sdown[half] for half in range(2)]
        sup = [albedo * below[half] for half in range(2)]
        result = jnp.zeros((WIDE, 128), jnp.float32)

        def settle(result, face, upper, shorter):
            long_net = [(up[half] - upper[half]) * planck_part[half] for half in range(2)]
            short_net = [sup[half] - shorter[half] for half in range(2)]
            long_sum = jnp.sum(long_net[0] + long_net[1], axis=1, keepdims=True)
            short_sum = jnp.sum(short_net[0] + short_net[1], axis=1, keepdims=True)
            result = jnp.where(lane == face, long_sum, result)
            return jnp.where(lane == SHORT_AT + face, short_sum, result)

        result = settle(result, LEVELS, down, below)
        for level in reversed(range(LEVELS)):
            planck = wide(fields, 96 + level)
            for half in range(2):
                up[half] = planck + held[level, half] * (up[half] - planck)
                sup[half] = held[level, 4 + half] * sup[half] + held[level, 6 + half]
            result = settle(
                result,
                level,
                [held[level, 2 + half] for half in range(2)],
                [held[level, 8 + half] for half in range(2)],
            )
        result = pltpu.roll(result, 127, 1) - result
        flag = jnp.where(step < COLS // 2 // WIDE, lit[0], lit[1]).astype(jnp.float32)
        is_long = lane < SHORT_AT
        thickness = jnp.where(is_long, fields, pltpu.roll(fields, SHORT_AT, 1))
        factor = jnp.where(is_long, 1.0 / 256.0, cosine * (flag / 224.0))
        keep = (lane % SHORT_AT < LEVELS) & (lane < 2 * SHORT_AT)
        heat[pl.ds(start, WIDE), :] = jnp.where(
            keep, result * factor / jnp.where(keep, thickness, 1.0), 0.0
        )
        return carry

    lax.fori_loop(0, COLS // WIDE, body, 0)


def two(row):
    return [jnp.broadcast_to(row[:, 0:128], (WIDE, 128)), jnp.broadcast_to(row[:, 128:256], (WIDE, 128))]


def short_row(ref, fill):
    row = ref[...]
    return jnp.concatenate([row, jnp.full((1, 32), fill, jnp.float32)], axis=1)


def exchange(axis, outgoing, incoming, send_sem, recv_sem):
    count = lax.axis_size(axis)
    me = lax.axis_index(axis)
    for step in range(1, count):
        peer = lax.rem(me + step, count)
        pltpu.make_async_remote_copy(
            src_ref=outgoing(peer),
            dst_ref=incoming(me),
            send_sem=send_sem,
            recv_sem=recv_sem,
            device_id={axis: peer},
            device_id_type=pl.DeviceIdType.MESH,
        ).start()


def await_all(axis, buffer, send_sem, recv_sem):
    whole = buffer.at[pl.ds(0, lax.axis_size(axis) - 1)]
    pltpu.make_async_copy(whole, whole, send_sem).wait()
    pltpu.make_async_copy(whole, whole, recv_sem).wait()


def load_tables(long_hbm, short_hbm, long_in, short_in, sems):
    copies = []
    for piece in range(4):
        part = pl.ds(piece * 1920, min(1920, NTAB - piece * 1920))
        copies.append(
            pltpu.make_async_copy(long_hbm.at[part], long_in.at[part], sems.at[piece])
        )
    for piece in range(2):
        part = pl.ds(piece * 112, 112)
        copies.append(
            pltpu.make_async_copy(short_hbm.at[part], short_in.at[part], sems.at[4 + piece])
        )
    return copies


def column_kernel(
    lit,
    targets,
    amount,
    scatter,
    cloud_path,
    planck,
    thickness,
    cosine,
    albedo,
    surface,
    weights,
    index,
    cloud_long,
    cloud_short,
    planck_part,
    ray,
    flux,
    long_hbm,
    short_hbm,
    returned,
    slot_out,
    table,
    long_in,
    short_in,
    rows_v,
    rows,
    lanes,
    kappa,
    state,
    heat,
    held,
    outgoing,
    middle,
    incoming,
    back_out,
    arrival,
    sems,
    send_sem,
    recv_sem,
):
    me = lax.axis_index("face") * ELEMS + lax.axis_index("elem")
    copies = load_tables(long_hbm, short_hbm, long_in, short_in, sems)
    for copy in copies:
        copy.start()
    face = lax.axis_index("face")
    elem = lax.axis_index("elem")
    barrier = pltpu.get_barrier_semaphore()
    for axis, count in (("face", FACES), ("elem", ELEMS)):
        for step in range(1, count):
            pl.semaphore_signal(
                barrier,
                inc=1,
                device_id={axis: lax.rem(lax.axis_index(axis) + step, count)},
                device_id_type=pl.DeviceIdType.MESH,
            )
    rows_v[...] = index[...] * 4
    row_copies = []
    for level in range(LEVELS):
        row_copies.append(
            pltpu.make_async_copy(rows_v.at[level], rows.at[pl.ds(level * COLS, COLS)], sems.at[6])
        )
    for copy in row_copies:
        copy.start()

    slot, position = slots_of(targets[pl.ds(2 * me, 2), :])
    fields = jnp.concatenate(
        [
            thickness[...],
            amount[...],
            scatter[...],
            cloud_path[...],
            planck[...],
            as_row(cosine[...]),
            as_row(albedo[...]),
            as_row(surface[...]),
            position,
            jnp.zeros((4, COLS), jnp.float32),
        ],
        axis=0,
    )
    chooser = onehot(slot == iota((COLS, COLS), 0).astype(jnp.float32))
    slot_out[...] = slot
    outgoing[...] = pick(chooser, fields, 1).reshape(FACES, ELEMS, 2, 128)
    own = pltpu.make_async_copy(outgoing.at[face], middle.at[face], sems.at[7])
    own.start()
    spread_weights(weights, lanes)
    for copy in copies[:4]:
        copy.wait()
    fill_long(long_in, table)
    pl.semaphore_wait(barrier, FACES + ELEMS - 2)
    exchange(
        "face", lambda k: outgoing.at[k], lambda k: middle.at[k], send_sem.at[0], recv_sem.at[0]
    )
    for copy in copies[4:]:
        copy.wait()
    fill_short(short_in, table)
    for copy in row_copies:
        copy.wait()
    steps = 3 * COLS // GROUP
    gather(rows, table, lanes, kappa, 0, steps // 6)
    own.wait()
    await_all("face", middle, send_sem.at[0], recv_sem.at[0])
    exchange(
        "elem", lambda k: middle.at[:, k], lambda k: incoming.at[k], send_sem.at[1], recv_sem.at[1]
    )
    own = pltpu.make_async_copy(middle.at[:, elem], incoming.at[elem], sems.at[7])
    own.start()
    gather(rows, table, lanes, kappa, steps // 6, steps)
    own.wait()
    await_all("elem", incoming, send_sem.at[1], recv_sem.at[1])
    got = incoming[...].reshape(COLS, 128)
    arrived = got[:, 123:124]
    arrival[...] = got
    state[...] = pick(onehot(to_row(arrived) == iota((COLS, COLS), 0).astype(jnp.float32)), got)
    params = (
        two(as_row(cloud_long[...])),
        two(as_row(planck_part[...])),
        two(short_row(cloud_short, 0.0) * 0.5),
        two(short_row(ray, 1.0) * 0.5),
        two(short_row(flux, 0.0)),
    )
    radiate(state, kappa, heat, lit, params, held)
    for rank in range(2):
        there = arrival[pl.ds(rank, COLS // 2, 2), :][:, 123:124]
        back = onehot(there == iota((COLS // 2, COLS), 1).astype(jnp.float32))
        found = pick(back, heat[...])
        both = found if rank == 0 else both + pltpu.roll(found, 64, 1)
    back_out[...] = both.reshape(COLS // 2, 1, 128)
    own = pltpu.make_async_copy(
        back_out.at[elem * FACES + face], returned.at[me], sems.at[7]
    )
    own.start()

    def send_one(step):
        peer = (me + step) & (FACES * ELEMS - 1)
        to_face = peer >> 4
        to_elem = peer & 15
        pltpu.make_async_remote_copy(
            src_ref=back_out.at[to_elem * FACES + to_face],
            dst_ref=returned.at[me],
            send_sem=send_sem.at[2],
            recv_sem=recv_sem.at[2],
            device_id=(to_face, to_elem),
            device_id_type=pl.DeviceIdType.MESH,
        ).start()

    def send_home(group, carry):
        for inner in range(9):
            send_one(group * 9 + inner + 1)
        return carry

    lax.fori_loop(0, 14, send_home, 0)
    send_one(127)
    own.wait()
    most = back_out.at[pl.ds(0, FACES * ELEMS - 1)]
    pltpu.make_async_copy(most, most, send_sem.at[2]).wait()
    pltpu.make_async_copy(most, most, recv_sem.at[2]).wait()


def home_kernel(returned, slot, long_out, short_out):
    place = to_column(slot[...])
    peer = jnp.floor(place * 0.5)
    home = onehot(peer == iota((COLS, COLS // 2), 1).astype(jnp.float32))
    both = pick(home, returned[...].reshape(COLS // 2, 128))
    final = jnp.where(place > 2.0 * peer, pltpu.roll(both, 64, 1), both).T
    long_out[...] = final[:LEVELS]
    short_out[...] = final[SHORT_AT:SHORT_AT + LEVELS]


def on_device(
    amount,
    scatter,
    cloud_path,
    planck,
    thickness,
    corner_weights,
    table_index,
    cosine,
    albedo,
    surface_source,
    stretch_map,
    sunlit,
    table_longwave,
    table_shortwave,
    cloud_longwave,
    cloud_shortwave,
    planck_fraction,
    rayleigh,
    solar_flux,
):
    anywhere = pl.BlockSpec(memory_space=pl.ANY)
    vector = pl.BlockSpec(memory_space=pltpu.VMEM)
    scalar = pl.BlockSpec(memory_space=pltpu.SMEM)
    field = jax.ShapeDtypeStruct((LEVELS, COLS), jnp.float32)
    by_face = pltpu.VMEM((FACES, ELEMS, 2, 128), jnp.float32)
    by_elem = pltpu.VMEM((ELEMS, FACES, 2, 128), jnp.float32)
    returned, slot = pl.pallas_call(
        column_kernel,
        out_shape=(
            jax.ShapeDtypeStruct((COLS // 2, 1, 128), jnp.float32),
            jax.ShapeDtypeStruct((1, COLS), jnp.float32),
        ),
        in_specs=[scalar] + [vector] * 16 + [anywhere] * 2,
        out_specs=(anywhere, vector),
        scratch_shapes=[
            pltpu.VMEM((NTAB * 4, 128), jnp.float32),
            pltpu.VMEM((NTAB, 256), jnp.bfloat16),
            pltpu.VMEM((256, NTAB), jnp.bfloat16),
            pltpu.VMEM((LEVELS, COLS), jnp.int32),
            pltpu.SMEM((LEVELS * COLS,), jnp.int32),
            pltpu.VMEM((2, 3 * COLS, 128), jnp.float32),
            pltpu.VMEM((12 * COLS * PITCH, 128), jnp.float32),
            pltpu.VMEM((COLS, 128), jnp.float32),
            pltpu.VMEM((COLS, 128), jnp.float32),
            pltpu.VMEM((LEVELS, 10, WIDE, 128), jnp.float32),
            by_face,
            by_face,
            by_elem,
            pltpu.VMEM((COLS // 2, 1, 128), jnp.float32),
            pltpu.VMEM((COLS, 128), jnp.float32),
            pltpu.SemaphoreType.DMA((8,)),
            pltpu.SemaphoreType.DMA((3,)),
            pltpu.SemaphoreType.DMA((3,)),
        ],
        compiler_params=pltpu.CompilerParams(
            collective_id=0, has_side_effects=True, vmem_limit_bytes=60 * 2**20
        ),
    )(
        sunlit,
        stretch_map.reshape(COLS, 128),
        amount,
        scatter,
        cloud_path,
        planck,
        thickness,
        cosine.reshape(2, 128),
        albedo.reshape(2, 128),
        surface_source.reshape(2, 128),
        corner_weights,
        table_index,
        cloud_longwave.reshape(2, 128),
        cloud_shortwave.reshape(1, 224),
        planck_fraction.reshape(2, 128),
        rayleigh.reshape(1, 224),
        solar_flux.reshape(1, 224),
        table_longwave,
        table_shortwave.T,
    )
    return pl.pallas_call(
        home_kernel,
        out_shape=(field, field),
        in_specs=[vector, vector],
        out_specs=(vector, vector),
    )(returned, slot)


def solution(mesh):
    columns = P(None, ("face", "elem"))
    single = P(("face", "elem"))
    in_specs = (
        (columns,) * 5
        + (P(None, None, ("face", "elem")), columns)
        + (single,) * 3
        + (P(), single)
        + (P(),) * 7
    )
    return jax.shard_map(
        on_device, mesh=mesh, in_specs=in_specs, out_specs=(columns, columns), check_vma=False
    )
```
